128 devices in a mesh: src: 16 (over y, z), win: 8 (over x, core).
Axes of the slice: x: 4, y: 4, z: 4, core: 2. Of those that a mesh axis runs over, the one named last changes fastest.
Arguments:
- src_design: float32 [65536, 5, 128], P(('src', 'win')), may hold values from -6 to 6
- att_comp: float32 [65536, 4, 128], P(('src', 'win')), may hold values from -6 to 6
- spline_phase: float32 [65536, 128], P(('src', 'win')), may hold values from 0 to 1
- knot_offset: int32 [65536, 128], P(('src', 'win')), may hold values from 0 to 60
- obs_weight: float32 [65536, 128], P(('src', 'win')), may hold values from 9.765625e-05 to 0.0009765625
- residual: float32 [65536, 128], P(('src', 'win')), may hold values from -220 to 220
- block_source: int32 [65536], P(('src', 'win')), may hold values from 0 to 4095, as said below
- block_window: int32 [65536], P(('src', 'win')), may hold values from 0 to 255, as said below
- send_list: int32 [2048, 64], P(('src', 'win')), may hold values from 0 to 511, as said below
- send_count: int32 [2048], P(('src', 'win')), may hold values from 0 to 64, as said below
Outputs:
- source_step: float32 [5, 4096], P(None, 'src')
- attitude_step: float32 [256, 256], P(('src', 'win'))
- final_residual: float32 [65536, 128], P(('src', 'win'))
The draws below stay inside these ranges and needn't reach their ends.
Inputs may be any that keep to these rules, and one draw needn't show every extreme that they name: `block_source`: Non-decreasing along the blocks of each device; the device at src index i names only sources i * 256 to (i + 1) * 256 - 1. `block_window`: window W is owned by the device whose flat index in src+win order is W // 2; every block names a window owned by a device of its own win index. `send_list`: row k of a device's lists names, in increasing order and as indices 0 to 511 into that device's blocks, its blocks whose windows the device at src index k of its win column owns; every block is named exactly once among the valid entries; entries past the count are 0. `send_count`: the counts of one device sum to 512; in every draw some owner of each win column receives exactly 64 blocks from every device of that column.
All inputs are finite; a program needn't handle non-finite values.
Results may differ from the reference program's by a relative error of at most 0.0003.
Values sent between devices are 32-bit elements; how exact they have to be, the bound alone decides.
No kernel may reach another device: no remote copies, remote signals or barrier semaphores. Data moves between devices by JAX's collectives and lax.ppermute only.
A program may use at most 192 MiB of HBM per device.

```python
import math
import jax
import jax.numpy as jnp
from jax import lax

OBS = 128
KNOTS = 64
WIN_SUB = 2
BLK_DEV = 512
SRC_DEV = 256
CAP = 64
BLOCKS = 65536
SOURCES = 4096
WINDOWS = 256
OBS_SRC = 2048
OBS_WIN = 32768
N_SRC = 16
N_WIN = 8


def block_layout(key):
    devices_all = N_SRC * N_WIN
    share = BLK_DEV // N_SRC
    column_keys = jax.random.split(jax.random.fold_in(key, 11), N_WIN)
    rank_order = jax.vmap(lambda one_key: jax.random.permutation(one_key, N_SRC))(column_keys)
    ranks = jnp.argsort(rank_order, axis=1).astype(jnp.int32)
    column = jnp.arange(devices_all) % N_WIN
    device_rank = ranks[column]
    base = jnp.where(device_rank == 0, 2 * share, jnp.where(device_rank == 1, 0, share))
    pair_index = (jnp.maximum(device_rank - 2, 0) // 2).astype(jnp.int32)
    pair_sign = jnp.where(device_rank % 2 == 0, 1, -1)
    moves = jax.random.randint(jax.random.fold_in(key, 12), (devices_all, N_SRC), 0, share // 2 + 1)
    moved = jnp.take_along_axis(moves, pair_index, axis=1)
    counts = (base + jnp.where(device_rank >= 2, pair_sign * moved, 0)).astype(jnp.int32)
    ends = jnp.cumsum(counts, axis=1)
    starts = ends - counts
    position = jnp.arange(BLK_DEV)
    owner_at = jnp.sum(position[None, :, None] >= ends[:, None, :], axis=2).astype(jnp.int32)
    shuffle_keys = jax.random.split(jax.random.fold_in(key, 13), devices_all)
    shuffles = jax.vmap(lambda one_key: jax.random.permutation(one_key, BLK_DEV))(shuffle_keys)
    owners = jnp.take_along_axis(owner_at, shuffles, axis=1)
    order = jnp.argsort(owners, axis=1, stable=True).astype(jnp.int32)
    slots = jnp.arange(CAP)
    wanted = jnp.minimum(starts[:, :, None] + slots[None, None, :], BLK_DEV - 1)
    listed = jnp.take_along_axis(order, wanted.reshape(devices_all, N_SRC * CAP), axis=1).reshape(devices_all, N_SRC, CAP)
    lists = jnp.where(slots[None, None, :] < counts[:, :, None], listed, 0).astype(jnp.int32)
    subs = jax.random.randint(jax.random.fold_in(key, 14), (devices_all, BLK_DEV), 0, WIN_SUB)
    windows = ((owners * N_WIN + column[:, None]) * WIN_SUB + subs).astype(jnp.int32)
    local = jnp.sort(jax.random.randint(jax.random.fold_in(key, 15), (devices_all, BLK_DEV), 0, SRC_DEV), axis=1)
    sources = (local + (jnp.arange(devices_all) // N_WIN)[:, None] * SRC_DEV).astype(jnp.int32)
    knots = jax.random.randint(jax.random.fold_in(key, 16), (BLOCKS, OBS), 0, KNOTS - 3).astype(jnp.int32)
    return (counts.reshape(-1), lists.reshape(devices_all * N_SRC, CAP), windows.reshape(-1), sources.reshape(-1), knots)


def rough_values(key, salt, rows):
    values = jax.random.normal(jax.random.fold_in(key, salt), (BLOCKS, rows, OBS), jnp.float32)
    return jnp.clip(values, -6.0, 6.0)


def phase_values(key):
    return jax.random.uniform(jax.random.fold_in(key, 41), (BLOCKS, OBS), jnp.float32, 0.0, 1.0)


def draw_src_design(key, part):
    return rough_values(key, 21, 5)


def draw_att_comp(key, part):
    return rough_values(key, 31, 4)


def draw_spline_phase(key, part):
    return phase_values(key)


def draw_knot_offset(key, part):
    return block_layout(key)[4]


def draw_block_source(key, part):
    return block_layout(key)[3]


def draw_block_window(key, part):
    return block_layout(key)[2]


def draw_send_list(key, part):
    return block_layout(key)[1]


def draw_send_count(key, part):
    return block_layout(key)[0]


def draw_residual(key, part):
    counts, lists, windows, sources, knots = block_layout(key)
    design = rough_values(key, 21, 5)
    comps = rough_values(key, 31, 4)
    phase = phase_values(key)
    source_truth = jax.random.normal(jax.random.fold_in(key, 51), (SOURCES, 5), jnp.float32)
    panel_truth = jax.random.normal(jax.random.fold_in(key, 52), (WINDOWS, KNOTS, 4), jnp.float32)
    source_truth = jnp.clip(source_truth, -4.0, 4.0)
    panel_truth = jnp.clip(panel_truth, -4.0, 4.0)
    panel_pad = jnp.concatenate([panel_truth, jnp.zeros((WINDOWS, 3, 4), jnp.float32)], axis=1)
    picked = source_truth[sources]
    signal = jnp.sum(design * picked[:, :, None], axis=1)
    square = phase * phase
    cube = square * phase
    rest = 1.0 - phase
    spline = [rest * rest * rest / 6.0, (3.0 * cube - 6.0 * square + 4.0) / 6.0, (-3.0 * cube + 3.0 * square + 3.0 * phase + 1.0) / 6.0, cube / 6.0]
    for first in range(4):
        values = panel_pad[windows[:, None], knots + first]
        signal = signal + spline[first] * jnp.sum(comps * jnp.transpose(values, (0, 2, 1)), axis=1)
    noise = jnp.clip(jax.random.normal(jax.random.fold_in(key, 53), (BLOCKS, OBS), jnp.float32), -6.0, 6.0)
    return signal + 0.5 * noise


def shard_levels(rng, extent, cuts, least, top_value):
    level, own = 1.0, jax.random.fold_in(rng, 6)
    for dim, shards_of in cuts:
        draws = jnp.exp(jax.random.uniform(jax.random.fold_in(own, dim), (shards_of,), jnp.float32, least / len(cuts), top_value / len(cuts)))
        level = level * jnp.repeat(draws, extent[dim] // shards_of).reshape([-1 if axis == dim else 1 for axis in range(len(extent))])
    return level


def setup_inputs(seed: int = 0) -> dict:
    streams_of = jax.random.split(jax.random.key(seed), 11)
    return {
        "src_design": draw_src_design(jax.random.fold_in(streams_of[10], 71), 0),
        "att_comp": draw_att_comp(jax.random.fold_in(streams_of[10], 71), 0),
        "spline_phase": draw_spline_phase(jax.random.fold_in(streams_of[10], 71), 0),
        "knot_offset": draw_knot_offset(jax.random.fold_in(streams_of[10], 71), 0),
        "obs_weight": jnp.clip(jnp.exp(math.log(0.0009765625) - 2.3025851 * jax.random.uniform(streams_of[4], (BLOCKS, OBS), jnp.float32) ** shard_levels(streams_of[4], (BLOCKS, OBS), ((0, 128),), -0.2, 0.2)), 9.765625145519152e-05, 0.0009765625),
        "residual": draw_residual(jax.random.fold_in(streams_of[10], 71), 0),
        "block_source": draw_block_source(jax.random.fold_in(streams_of[10], 71), 0),
        "block_window": draw_block_window(jax.random.fold_in(streams_of[10], 71), 0),
        "send_list": draw_send_list(jax.random.fold_in(streams_of[10], 71), 0),
        "send_count": draw_send_count(jax.random.fold_in(streams_of[10], 71), 0),
    }


def spline_weights(phase):
    square = phase * phase
    cube = square * phase
    rest = 1.0 - phase
    return [rest * rest * rest / 6.0, (3.0 * cube - 6.0 * square + 4.0) / 6.0, (-3.0 * cube + 3.0 * square + 3.0 * phase + 1.0) / 6.0, cube / 6.0]

def features(phase, comps, weight, resid_one):
    spline = spline_weights(phase)
    pairs = (comps[:, :, None, :] * comps[:, None, :, :]).reshape(comps.shape[0], 16, comps.shape[2])
    weighted_pairs = weight[:, None, :] * pairs
    slots = []
    for spacing in range(4):
        for first in range(4 - spacing):
            slots.append(weighted_pairs * (spline[first] * spline[first + spacing])[:, None, :])
    weighted_resid = weight * resid_one
    for first in range(4):
        slots.append((weighted_resid * spline[first])[:, None, :] * comps)
    return jnp.concatenate(slots, axis=1)

def shifted(values, amount):
    if amount == 0:
        return values
    padding = jnp.zeros_like(values[:, :amount])
    return jnp.concatenate([padding, values[:, :-amount]], axis=1)

def solve_panels(totals, prior):
    count = totals.shape[0]
    totals = totals.reshape(count, KNOTS, 176)
    bands = []
    slot_index = 0
    for spacing in range(4):
        band = jnp.zeros((count, KNOTS, 16), jnp.float32)
        for first in range(4 - spacing):
            band = band + shifted(totals[:, :, slot_index * 16:(slot_index + 1) * 16], first)
            slot_index += 1
        bands.append(band.reshape(count, KNOTS, 4, 4))
    right = jnp.zeros((count, KNOTS, 4), jnp.float32)
    for first in range(4):
        right = right + shifted(totals[:, :, 160 + first * 4:164 + first * 4], first)
    right = right.reshape(count, KNOTS * 4)
    dense = jnp.zeros((count, KNOTS, 4, KNOTS, 4), jnp.float32)
    for spacing in range(4):
        stepper = jnp.eye(KNOTS, k=spacing, dtype=jnp.float32)
        dense = dense + bands[spacing][:, :, :, None, :] * stepper[None, :, None, :, None]
        if spacing > 0:
            dense = dense + bands[spacing].transpose(0, 3, 1, 2)[:, None] * stepper.T[None, :, None, :, None]
    normal = dense.reshape(count, KNOTS * 4, KNOTS * 4) + prior * jnp.eye(KNOTS * 4, dtype=jnp.float32)[None]
    factor = jnp.linalg.cholesky(normal)
    return jax.scipy.linalg.cho_solve((factor, True), right[:, :, None])[:, :, 0]

def source_stats(design, weight, resid):
    weighted = design * weight[:, None, :]
    cross = jnp.einsum('bpo,bqo->bpq', weighted, design, precision=lax.Precision.HIGHEST)
    right = jnp.einsum('bpo,bo->bp', weighted, resid, precision=lax.Precision.HIGHEST)
    return jnp.concatenate([cross.reshape(design.shape[0], 25), right], axis=1)

def solve_five(totals):
    factor = {}
    for across in range(5):
        for within in range(across + 1):
            entry = totals[across * 5 + within]
            if across == within:
                entry = entry + 1.0
            for before in range(within):
                entry = entry - factor[across, before] * factor[within, before]
            if across == within:
                factor[across, within] = jnp.sqrt(entry)
            else:
                factor[across, within] = entry / factor[within, within]
    forward = []
    for across in range(5):
        entry = totals[25 + across]
        for before in range(across):
            entry = entry - factor[across, before] * forward[before]
        forward.append(entry / factor[across, across])
    backward = [None] * 5
    for across in range(4, -1, -1):
        entry = forward[across]
        for later in range(across + 1, 5):
            entry = entry - factor[later, across] * backward[later]
        backward[across] = entry / factor[across, across]
    return jnp.stack(backward, axis=0)

def reference(src_design, att_comp, spline_phase, knot_offset, obs_weight, residual, block_source, block_window, send_list, send_count):
    stats = source_stats(src_design, obs_weight, residual)
    totals = jax.ops.segment_sum(stats, block_source, num_segments=SOURCES).T
    source_step = solve_five(totals)
    per_block = source_step.T[block_source]
    resid_one = residual - lax.optimization_barrier(jnp.sum(src_design * per_block[:, :, None], axis=1))
    valid = (jnp.arange(CAP)[None, :] < send_count[:, None]).astype(jnp.float32)
    owner_device = (jnp.arange(send_list.shape[0]) // N_SRC).astype(jnp.int32)
    named = owner_device[:, None] * BLK_DEV + send_list
    multiple = jax.ops.segment_sum(valid.reshape(-1), named.reshape(-1).astype(jnp.int32), num_segments=BLOCKS)
    weight_att = obs_weight * multiple[:, None]
    group = 256
    turns = BLOCKS // group

    def one_group(totals_att, pieces):
        phase_g, comps_g, weight_g, resid_g, knots_g, window_g = pieces
        feats = features(phase_g, comps_g, weight_g, resid_g)
        rows_all = feats.transpose(0, 2, 1).reshape(group * OBS, 176)
        segment = (window_g[:, None] * KNOTS + knots_g).reshape(-1).astype(jnp.int32)
        return (totals_att + jax.ops.segment_sum(rows_all, segment, num_segments=WINDOWS * KNOTS), None)
    pieces = (spline_phase.reshape(turns, group, OBS), att_comp.reshape(turns, group, 4, OBS), weight_att.reshape(turns, group, OBS), resid_one.reshape(turns, group, OBS), knot_offset.reshape(turns, group, OBS), block_window.reshape(turns, group))
    start_totals = jnp.zeros((WINDOWS * KNOTS, 176), jnp.float32)
    totals_att, unused = lax.scan(one_group, start_totals, pieces)
    prior = 0.005 * OBS_WIN / OBS_SRC
    attitude_step = solve_panels(totals_att.reshape(WINDOWS, KNOTS * 176), prior)
    grid = jnp.concatenate([attitude_step.reshape(WINDOWS, KNOTS, 4), jnp.zeros((WINDOWS, 3, 4), jnp.float32)], axis=1)
    spline = spline_weights(spline_phase)
    correction = jnp.zeros_like(residual)
    for first in range(4):
        values = grid[block_window[:, None], knot_offset + first]
        summed = lax.optimization_barrier(jnp.sum(att_comp * jnp.transpose(values, (0, 2, 1)), axis=1))
        correction = correction + spline[first] * summed
    return (source_step, attitude_step, resid_one - correction)
```

```python
import jax
import jax.numpy as jnp
from jax import lax
from jax.experimental import pallas as pl
from jax.experimental.pallas import tpu as pltpu
from jax.sharding import PartitionSpec as P

OBS = 128
KNOTS = 64
WIN_SUB = 2
BLK_DEV = 512
SRC_DEV = 256
N_SRC = 16
N_COL = N_SRC * WIN_SUB
HALF = 30
PAIRS = [(p, q) for p in range(4) for q in range(p, 4)]
PAIR_ROWS = 8 * len(PAIRS)
RIGHT_ROWS = 16
ROWS = PAIR_ROWS + RIGHT_ROWS
STAT_ROWS = 24
F32 = jnp.float32
BF16 = jnp.bfloat16
NT = (((1,), (1,)), ((), ()))
SPLINE = [
    [1 / 6, 0.0, 0.0, 0.0],
    [4 / 6, 12 / 6, 6 / 6, 1 / 6],
    [1 / 6, 6 / 6, 12 / 6, 4 / 6],
    [0.0, 0.0, 0.0, 1 / 6],
]


def iota(shape, dim):
    return lax.broadcasted_iota(jnp.int32, shape, dim)


def split2(values):
    high = values.astype(BF16)
    return high, (values - high.astype(F32)).astype(BF16)


def split3(values):
    high = values.astype(BF16)
    rest = values - high.astype(F32)
    mid = rest.astype(BF16)
    return high, mid, (rest - mid.astype(F32)).astype(BF16)


def spline_weights(phase):
    square = phase * phase
    cube = square * phase
    rest = 1.0 - phase
    return [
        rest * rest * rest * (1.0 / 6.0),
        (3.0 * cube - 6.0 * square + 4.0) * (1.0 / 6.0),
        (-3.0 * cube + 3.0 * square + 3.0 * phase + 1.0) * (1.0 / 6.0),
        cube * (1.0 / 6.0),
    ]


def params(megabytes):
    return pltpu.CompilerParams(vmem_limit_bytes=megabytes * 1024 * 1024)


VMEM = pl.BlockSpec(memory_space=pltpu.VMEM)
SMEM = pl.BlockSpec(memory_space=pltpu.SMEM)


def stats_kernel(design_ref, weight_ref, resid_ref, source_ref, out_ref, sums_ref):
    rows = 32
    lane = iota((rows, OBS), 1)

    def one_group(group, carry):
        at = pl.ds(pl.multiple_of(group * rows, rows), rows)
        weight = weight_ref[at, :]
        design = [design_ref[p, at, :] for p in range(5)]
        resid = resid_ref[at, :]
        weighted = [weight * design[p] for p in range(5)]
        packed = jnp.zeros((rows, OBS), F32)
        slot = 0
        for p in range(5):
            for q in range(p + 1):
                total = jnp.sum(weighted[p] * design[q], axis=1, keepdims=True)
                packed = jnp.where(lane == slot, total, packed)
                slot += 1
        for p in range(5):
            total = jnp.sum(weighted[p] * resid, axis=1, keepdims=True)
            packed = jnp.where(lane == slot, total, packed)
            slot += 1
        sums_ref[at, :] = packed
        return carry

    lax.fori_loop(0, BLK_DEV // rows, one_group, 0)
    local = jnp.bitwise_and(source_ref[...], SRC_DEV - 1)
    hot = (iota((SRC_DEV, BLK_DEV), 0) == local).astype(F32).astype(BF16)
    total = jnp.zeros((SRC_DEV, OBS), F32)
    for piece in split3(sums_ref[...]):
        total = total + jnp.dot(hot, piece, preferred_element_type=F32)
    out_ref[...] = total.T[:STAT_ROWS]


def source_sums(design, weight, resid, source_row):
    return pl.pallas_call(
        stats_kernel,
        out_shape=jax.ShapeDtypeStruct((STAT_ROWS, SRC_DEV), F32),
        in_specs=[VMEM] * 4,
        out_specs=VMEM,
        scratch_shapes=[pltpu.VMEM((BLK_DEV, OBS), F32)],
        compiler_params=params(16),
        name="source_sums",
    )(design, weight, resid, source_row)


def column_window(window_ref, block):
    window = window_ref[block]
    return lax.shift_right_logical(window, 4) * 2 + jnp.bitwise_and(window, 1)


def normals_kernel(
    comp_ref,
    phase_ref,
    knot_ref,
    weight_ref,
    list_ref,
    count_ref,
    window_ref,
    out_ref,
    watt_ref,
    poly_ref,
    pair_ref,
    total_ref,
):
    named = jnp.zeros((16, BLK_DEV // 8), F32)
    capacity = list_ref.shape[1]
    slot = iota((1, capacity), 1)
    for owner in range(N_SRC):
        entry = jnp.where(slot < count_ref[owner], list_ref[owner : owner + 1, :], -1)
        group_hot = iota((BLK_DEV // 8, capacity), 0) == lax.shift_right_arithmetic(entry, 3)
        place_hot = iota((16, capacity), 0) == jnp.where(entry < 0, -1, jnp.bitwise_and(entry, 7))
        named = named + lax.dot_general(
            place_hot.astype(F32).astype(BF16),
            group_hot.astype(F32).astype(BF16),
            NT,
            preferred_element_type=F32,
        )
    named = jnp.concatenate([named[:8], jnp.zeros((8, OBS - BLK_DEV // 8), F32)], axis=1)

    def prepare(group, carry):
        at = pl.ds(pl.multiple_of(group * 8, 8), 8)
        phase = phase_ref[at, :]
        rest = 1.0 - phase
        up = [None, phase, phase * phase, None]
        down = [None, rest, rest * rest, None]
        up[3] = up[2] * phase
        down[3] = down[2] * rest
        poly = [
            down[3] * down[3],
            phase * (down[3] * down[2]),
            up[2] * (down[2] * down[2]),
            up[3] * down[3],
            (up[2] * up[2]) * down[2],
            (up[3] * up[2]) * rest,
            up[3] * up[3],
            jnp.zeros_like(phase),
        ]
        for k in range(8):
            poly_ref[pl.ds(group * 64 + k, 8, stride=8), :] = poly[k]
        times = jnp.take_along_axis(named, jnp.full((8, OBS), group, jnp.int32), axis=1)
        weight = weight_ref[at, :] * times
        watt_ref[at, :] = weight
        comps = [comp_ref[pl.ds(group * 32 + p, 8, stride=4), :] for p in range(4)]
        weighted = [weight * comps[p] for p in range(4)]
        for i, (p, q) in enumerate(PAIRS):
            pair_ref[i, at, :] = weighted[p] * comps[q]
        return carry

    lax.fori_loop(0, BLK_DEV // 8, prepare, 0, unroll=2)
    total_ref[...] = jnp.zeros_like(total_ref)
    knot_iota = iota((KNOTS, OBS), 0)
    unrolled = 16

    def one_group(group, carry):
        for i in range(unrolled):
            block = group * unrolled + i
            poly = poly_ref[pl.ds(pl.multiple_of(block * 8, 8), 8), :]
            terms = jnp.concatenate(
                [poly * pair_ref[n, pl.ds(block, 1), :] for n in range(len(PAIRS))], axis=0
            )
            high, low = split2(terms)
            hot = (knot_iota == knot_ref[pl.ds(block, 1), :]).astype(F32).astype(BF16)
            summed = lax.dot_general(
                jnp.concatenate([high, low], axis=1),
                jnp.concatenate([hot, hot], axis=1),
                NT,
                preferred_element_type=F32,
            )
            at = column_window(window_ref, block)
            total_ref[at] = total_ref[at] + summed
        return carry

    lax.fori_loop(0, BLK_DEV // unrolled, one_group, 0)
    for owner in range(N_SRC):
        out_ref[owner, :PAIR_ROWS, :] = jnp.concatenate(
            [total_ref[2 * owner], total_ref[2 * owner + 1]], axis=1
        )
        out_ref[owner, PAIR_ROWS:, :] = jnp.zeros((RIGHT_ROWS, OBS), F32)


def normal_sums(comps, phase, knots, weight, lists, counts, window):
    return pl.pallas_call(
        normals_kernel,
        out_shape=(
            jax.ShapeDtypeStruct((N_SRC, ROWS, OBS), F32),
            jax.ShapeDtypeStruct((BLK_DEV, OBS), F32),
        ),
        in_specs=[VMEM] * 5 + [SMEM] * 2,
        out_specs=(VMEM, VMEM),
        scratch_shapes=[
            pltpu.VMEM((BLK_DEV * 8, OBS), F32),
            pltpu.VMEM((len(PAIRS), BLK_DEV, OBS), F32),
            pltpu.VMEM((N_COL, PAIR_ROWS, KNOTS), F32),
        ],
        compiler_params=params(32),
        cost_estimate=pl.CostEstimate(flops=3_000_000_000, bytes_accessed=4_000_000, transcendentals=0),
        name="normal_sums",
    )(comps, phase, knots, weight, lists, counts, window)


def solve_five(totals):
    def entry_at(across, within):
        row = across * (across + 1) // 2 + within
        return totals[row : row + 1, :]

    factor = {}
    inverse = {}
    for across in range(5):
        for within in range(across + 1):
            entry = entry_at(across, within)
            if across == within:
                entry = entry + 1.0
            for before in range(within):
                entry = entry - factor[across, before] * factor[within, before]
            if across == within:
                inverse[across] = 1.0 / jnp.sqrt(entry)
            else:
                factor[across, within] = entry * inverse[within]
    forward = []
    for across in range(5):
        entry = totals[15 + across : 16 + across, :]
        for before in range(across):
            entry = entry - factor[across, before] * forward[before]
        forward.append(entry * inverse[across])
    backward = [None] * 5
    for across in range(4, -1, -1):
        entry = forward[across]
        for later in range(across + 1, 5):
            entry = entry - factor[later, across] * backward[later]
        backward[across] = entry * inverse[across]
    return backward


def rights_kernel(
    own_ref,
    near_ref,
    far_ref,
    cross_ref,
    design_ref,
    resid_ref,
    watt_ref,
    comp_ref,
    phase_ref,
    knot_ref,
    source_ref,
    window_ref,
    sums_in_ref,
    step_ref,
    first_ref,
    sums_ref,
    column_ref,
    term_ref,
    total_ref,
    right_ref,
    sem,
):
    totals = (own_ref[...] + near_ref[...]) + (far_ref[...] + cross_ref[...])
    step = solve_five(totals)
    for p in range(5):
        step_ref[p : p + 1, :] = step[p]
    stacked = jnp.concatenate(step + [jnp.zeros((3, SRC_DEV), F32)], axis=0)
    pieces = jnp.concatenate(list(split3(stacked)) + [jnp.zeros((8, SRC_DEV), BF16)], axis=0)
    local = jnp.bitwise_and(source_ref[...], SRC_DEV - 1)
    hot = (iota((SRC_DEV, BLK_DEV), 0) == local).astype(F32).astype(BF16)
    picked = jnp.dot(pieces, hot, preferred_element_type=F32)
    picked = picked[:8] + picked[8:16] + picked[16:24]
    column_ref[...] = jnp.concatenate([picked, jnp.zeros((OBS - 8, BLK_DEV), F32)], axis=0).T

    def prepare(group, carry):
        at = pl.ds(pl.multiple_of(group * 8, 8), 8)
        columns = column_ref[at, :]
        fitted = jnp.zeros((8, OBS), F32)
        for p in range(5):
            fitted = fitted + design_ref[p, at, :] * columns[:, p : p + 1]
        first = resid_ref[at, :] - fitted
        first_ref[at, :] = first
        weighted = watt_ref[at, :] * first
        spline = spline_weights(phase_ref[at, :])
        comps = [comp_ref[pl.ds(group * 32 + p, 8, stride=4), :] for p in range(4)]
        for m in range(4):
            scaled = weighted * spline[m]
            for p in range(4):
                term_ref[pl.ds(group * 128 + 4 * m + p, 8, stride=16), :] = scaled * comps[p]
        return carry

    lax.fori_loop(0, BLK_DEV // 8, prepare, 0, unroll=2)
    total_ref[...] = jnp.zeros_like(total_ref)
    knot_iota = iota((KNOTS, OBS), 0)
    unrolled = 16

    def one_group(group, carry):
        for i in range(unrolled):
            block = group * unrolled + i
            terms = term_ref[pl.ds(pl.multiple_of(block * 16, 16), 16), :]
            high, low = split2(terms)
            hot = (knot_iota == knot_ref[pl.ds(block, 1), :]).astype(F32).astype(BF16)
            summed = lax.dot_general(
                jnp.concatenate([high, low], axis=1),
                jnp.concatenate([hot, hot], axis=1),
                NT,
                preferred_element_type=F32,
            )
            at = column_window(window_ref, block)
            total_ref[at] = total_ref[at] + summed
        return carry

    lax.fori_loop(0, BLK_DEV // unrolled, one_group, 0)
    for owner in range(N_SRC):
        right_ref[owner] = jnp.concatenate([total_ref[2 * owner], total_ref[2 * owner + 1]], axis=1)
    copy = pltpu.make_async_copy(right_ref, sums_ref.at[:, PAIR_ROWS:ROWS, :], sem)
    copy.start()
    copy.wait()


def right_sums(parts, design, resid, watt, comps, phase, knots, source_row, window, sums):
    return pl.pallas_call(
        rights_kernel,
        out_shape=(
            jax.ShapeDtypeStruct((5, SRC_DEV), F32),
            jax.ShapeDtypeStruct((BLK_DEV, OBS), F32),
            jax.ShapeDtypeStruct((N_SRC, ROWS, OBS), F32),
        ),
        in_specs=[VMEM] * 11 + [SMEM, pl.BlockSpec(memory_space=pl.ANY)],
        out_specs=(VMEM, VMEM, pl.BlockSpec(memory_space=pl.ANY)),
        scratch_shapes=[
            pltpu.VMEM((BLK_DEV, OBS), F32),
            pltpu.VMEM((BLK_DEV * 16, OBS), F32),
            pltpu.VMEM((N_COL, RIGHT_ROWS, KNOTS), F32),
            pltpu.VMEM((N_SRC, RIGHT_ROWS, OBS), F32),
            pltpu.SemaphoreType.DMA,
        ],
        input_output_aliases={12: 2},
        compiler_params=params(32),
        name="right_sums",
    )(*parts, design, resid, watt, comps, phase, knots, source_row, window, sums)


def roll(values, amount, axis):
    size = values.shape[axis]
    return pltpu.roll(values, amount % size, axis) if amount % size else values


def convolved(first, second):
    out = [0.0] * 7
    for i in range(4):
        for j in range(4):
            out[i + j] += SPLINE[first][i] * SPLINE[second][j]
    return out


def solve_kernel(prior, got_ref, out_ref, sum_ref, work_ref):
    total = got_ref[0]
    for other in range(1, N_SRC):
        total = total + got_ref[other]
    sum_ref[...] = total
    lane8 = iota((8, OBS), 1)
    sublane8 = iota((8, OBS), 0)
    low_terms = [sum_ref[pl.ds(k, 8, stride=8), :] for k in range(7)]
    high_terms = [sum_ref[pl.ds(64 + k, 2, stride=8), :] for k in range(7)]
    bands = []
    for spacing in range(4):
        low = jnp.zeros((8, OBS), F32)
        high = jnp.zeros((2, OBS), F32)
        for first in range(4 - spacing):
            weights = convolved(first, first + spacing)
            low_slot = jnp.zeros((8, OBS), F32)
            high_slot = jnp.zeros((2, OBS), F32)
            for k in range(7):
                if weights[k] != 0.0:
                    low_slot = low_slot + weights[k] * low_terms[k]
                    high_slot = high_slot + weights[k] * high_terms[k]
            low = low + roll(low_slot, first, 1)
            high = high + roll(high_slot, first, 1)
        rows = [low[i : i + 1] for i in range(8)] + [high[i : i + 1] for i in range(2)]
        if spacing == 0:
            rows = [row + prior if PAIRS[i][0] == PAIRS[i][1] else row for i, row in enumerate(rows)]
        index = {}
        for i, (p, q) in enumerate(PAIRS):
            index[p, q] = index[q, p] = i
        full = [rows[index[p, q]] for p in range(4) for q in range(4)]
        bands.append([jnp.concatenate(full[:8], axis=0), jnp.concatenate(full[8:], axis=0)])
    right = sum_ref[PAIR_ROWS : PAIR_ROWS + 4, :]
    for first in range(1, 4):
        right = right + roll(sum_ref[PAIR_ROWS + 4 * first : PAIR_ROWS + 4 * first + 4, :], first, 1)
    right = jnp.concatenate([right, right], axis=0)

    place = jnp.bitwise_and(lane8, 31)
    window_at = jnp.bitwise_and(lane8, 64)
    is_down = jnp.bitwise_and(lane8, 32) != 0

    def arranged(values, spacing, base):
        step = place + base
        up_index = jnp.minimum(window_at + step, OBS - 1)
        down_index = jnp.maximum(window_at + KNOTS - 1 - step, 0)
        up = jnp.take_along_axis(roll(values, spacing, 1), up_index, axis=1)
        down = jnp.take_along_axis(values, down_index, axis=1)
        down = jnp.where(step - spacing >= HALF, 0.0, down)
        return jnp.where(is_down, down, up)

    stream = [arranged(bands[d][h], d, 0) for d in range(4) for h in range(2)] + [
        arranged(right, 0, 0)
    ]
    tail = [arranged(bands[d][h], d, 32) for d in range(4) for h in range(2)] + [
        arranged(right, 0, 32)
    ]
    lower = sublane8 < 4

    def insert(front, target, pieces, slot, present):
        def part(d, p, half):
            values = pieces[2 * d + p // 2]
            return values if p % 2 == half else roll(values, 4, 0)

        for d in range(1, present + 1):
            other = (slot - d) % 4
            for q in range(4):
                old = front[other * 4 + q]
                fresh = part(d, q, slot % 2)
                keep = lower if slot % 2 == 1 else jnp.logical_not(lower)
                old[slot // 2] = jnp.where(keep, old[slot // 2], fresh)
        for p in range(4):
            halves = []
            for h in range(2):
                both = []
                for spot in range(2):
                    d = (slot - (2 * h + spot)) % 4
                    both.append(part(d, p, spot) if d <= present else jnp.zeros((8, OBS), F32))
                halves.append(jnp.where(lower, both[0], both[1]))
            front[slot * 4 + p] = halves
        keep = lower if slot % 2 == 1 else jnp.logical_not(lower)
        target[slot // 2] = jnp.where(keep, target[slot // 2], pieces[8])

    def eliminate(front, target, slot, gone):
        for p in range(4):
            row = slot * 4 + p
            half, at = row // 8, row % 8
            column = front[row]
            inverse = 1.0 / column[half][at : at + 1, :]
            gone = gone | {row}
            for c in [c for c in range(16) if c not in gone] + [16]:
                values = target if c == 16 else front[c]
                factor = values[half][at : at + 1, :] * inverse
                for h in range(2):
                    values[h] = values[h] - column[h] * factor
                values[half] = jnp.where(sublane8 == at, factor, values[half])
        return gone

    def save(front, target, slot, step):
        for r in range(1, 4):
            for q in range(4):
                work_ref[step * 13 + (r - 1) * 4 + q] = front[(slot + r) % 4 * 4 + q][slot // 2]
        work_ref[step * 13 + 12] = target[slot // 2]

    zero = jnp.zeros((8, OBS), F32)
    front = [[zero, zero] for _ in range(16)]
    target = [zero, zero]
    for step in range(4):
        insert(front, target, stream, step, step)
        stream = [roll(values, -1, 1) for values in stream]

    def four_knots(turn, carry):
        front = [list(pair) for pair in carry[0]]
        target = list(carry[1])
        stream = list(carry[2])
        for slot in range(4):
            eliminate(front, target, slot, frozenset())
            save(front, target, slot, turn * 4 + slot)
            insert(front, target, stream, slot, 3)
            stream = [roll(values, -1, 1) for values in stream]
        return (front, target, stream)

    front, target, stream = lax.fori_loop(0, 7, four_knots, (front, target, stream))
    for slot in range(2):
        eliminate(front, target, slot, frozenset())
        save(front, target, slot, 28 + slot)
        insert(front, target, tail, slot, 3)
        tail = [roll(values, -1, 1) for values in tail]

    mirror = jnp.bitwise_xor(lane8, 32)

    def mirrored(values):
        return jnp.take_along_axis(roll(values, 4, 0), mirror, axis=1)

    front = [
        [front[a * 4 + p][h] + mirrored(front[(3 - a) * 4 + p][1 - h]) for h in range(2)]
        for a in range(4)
        for p in range(4)
    ]
    target = [target[h] + mirrored(target[1 - h]) for h in range(2)]
    gone = frozenset()
    for slot in (2, 3, 0, 1):
        gone = eliminate(front, target, slot, gone)

    first_lane = place == 0

    def emit(result, answer, slot):
        values = answer[slot // 2]
        values = values if slot % 2 == 0 else roll(values, 4, 0)
        return jnp.where(first_lane, values, roll(result, 1, 1))

    def back(answer, slot, step):
        half = slot // 2
        sums = [work_ref[step * 13 + 12], zero]
        for r in (3, 2, 1):
            other = (slot + r) % 4
            for q in range(4):
                at = other % 2 * 4 + q
                sums[q % 2] = sums[q % 2] - work_ref[step * 13 + (r - 1) * 4 + q] * (
                    answer[other // 2][at : at + 1, :]
                )
        fresh = sums[0] + sums[1]
        keep = lower if slot % 2 == 1 else jnp.logical_not(lower)
        answer[half] = jnp.where(keep, answer[half], fresh)

    answer = list(target)
    result = emit(zero, answer, 3)
    result = emit(result, answer, 2)
    for slot in (1, 0):
        back(answer, slot, 28 + slot)
        result = emit(result, answer, slot)

    def four_back(turn, carry):
        answer = list(carry[0])
        result = carry[1]
        for slot in (3, 2, 1, 0):
            back(answer, slot, (6 - turn) * 4 + slot)
            result = emit(result, answer, slot)
        return (answer, result)

    answer, result = lax.fori_loop(0, 7, four_back, (answer, result))
    knot = jnp.bitwise_and(lane8, KNOTS - 1)
    from_lane = jnp.where(knot < 32, lane8, window_at + 32 + KNOTS - 1 - knot)
    panel = jnp.take_along_axis(result, from_lane, axis=1)
    for owner in range(N_SRC):
        out_ref[owner] = panel


def solve_panels(got, prior):
    def body(*refs):
        solve_kernel(prior, *refs)

    return pl.pallas_call(
        body,
        out_shape=jax.ShapeDtypeStruct((N_SRC, 8, OBS), F32),
        in_specs=[VMEM],
        out_specs=VMEM,
        scratch_shapes=[
            pltpu.VMEM((ROWS, OBS), F32),
            pltpu.VMEM((HALF * 13, 8, OBS), F32),
        ],
        compiler_params=params(16),
        name="solve_panels",
    )(got)


def final_kernel(panel_ref, comp_ref, phase_ref, knot_ref, first_ref, window_ref, out_ref, table_ref):
    for owner in range(N_SRC):
        tile = panel_ref[owner]
        table_ref[owner * 16 : owner * 16 + 8, :] = tile
        table_ref[owner * 16 + 8 : owner * 16 + 16, :] = roll(tile, 64, 1)

    def one_group(group, carry):
        at = pl.ds(pl.multiple_of(group * 8, 8), 8)
        knots = knot_ref[at, :]
        spline = spline_weights(phase_ref[at, :])
        starts = [column_window(window_ref, group * 8 + i) * 8 for i in range(8)]
        correction = [jnp.zeros((8, OBS), F32) for _ in range(4)]
        for p in range(4):
            table = jnp.concatenate([table_ref[pl.ds(start + p, 1), :] for start in starts], axis=0)
            comps = comp_ref[pl.ds(group * 32 + p, 8, stride=4), :]
            for m in range(4):
                correction[m] = correction[m] + comps * jnp.take_along_axis(table, knots + m, axis=1)
        total = spline[0] * correction[0]
        for m in range(1, 4):
            total = total + spline[m] * correction[m]
        out_ref[at, :] = first_ref[at, :] - total
        return carry

    lax.fori_loop(0, BLK_DEV // 8, one_group, 0, unroll=4)


def final_residual(panels, comps, phase, knots, first, window):
    return pl.pallas_call(
        final_kernel,
        out_shape=jax.ShapeDtypeStruct((BLK_DEV, OBS), F32),
        in_specs=[VMEM] * 5 + [SMEM],
        out_specs=VMEM,
        scratch_shapes=[pltpu.VMEM((N_COL * 8, OBS), F32)],
        compiler_params=params(16),
        name="final_residual",
    )(panels, comps, phase, knots, first, window)


def shards(
    src_design,
    att_comp,
    spline_phase,
    knot_offset,
    obs_weight,
    residual,
    block_source,
    block_window,
    send_list,
    send_count,
):
    n_win = lax.axis_size("win")
    design = src_design.transpose(1, 0, 2)
    comps = att_comp.reshape(BLK_DEV * 4, OBS)
    source_row = block_source.reshape(1, BLK_DEV)
    obs_src = OBS * BLK_DEV * n_win // SRC_DEV
    obs_win = OBS * BLK_DEV // WIN_SUB
    prior = 0.005 * obs_win / obs_src

    def swap(values, bit):
        return lax.ppermute(values, "win", [(i, i ^ bit) for i in range(n_win)])

    stats = source_sums(design, obs_weight, residual, source_row)
    stats = stats + swap(stats, 1)
    parts = (stats, swap(stats, 2), swap(stats, 4), swap(stats, 6))
    sums, watt = normal_sums(
        comps, spline_phase, knot_offset, obs_weight, send_list, send_count, block_window
    )
    source_step, first, sums = right_sums(
        parts,
        design,
        residual,
        watt,
        comps,
        spline_phase,
        knot_offset,
        source_row,
        block_window,
        sums,
    )
    got = lax.all_to_all(sums, "src", split_axis=0, concat_axis=0, tiled=True)
    own_panels = solve_panels(got, prior)
    panels = lax.all_to_all(own_panels, "src", split_axis=0, concat_axis=0, tiled=True)
    attitude_step = (
        own_panels[0, :4].reshape(4, WIN_SUB, KNOTS).transpose(1, 2, 0).reshape(WIN_SUB, KNOTS * 4)
    )
    last = final_residual(panels, comps, spline_phase, knot_offset, first, block_window)
    return (source_step, attitude_step, last)


def solution(mesh):
    return jax.shard_map(
        shards,
        mesh=mesh,
        in_specs=(
            P(("src", "win"), None, None),
            P(("src", "win"), None, None),
            P(("src", "win"), None),
            P(("src", "win"), None),
            P(("src", "win"), None),
            P(("src", "win"), None),
            P(("src", "win")),
            P(("src", "win")),
            P(("src", "win"), None),
            P(("src", "win")),
        ),
        out_specs=(P(None, "src"), P(("src", "win"), None), P(("src", "win"), None)),
        check_vma=False,
    )
```

```python
import jax
import jax.numpy as jnp
from jax import lax
from jax.experimental import pallas as pl
from jax.experimental.pallas import tpu as pltpu
from jax.sharding import PartitionSpec as P

OBS = 128
KNOTS = 64
WIN_SUB = 2
BLK_DEV = 512
SRC_DEV = 256
N_SRC = 16
N_COL = N_SRC * WIN_SUB
HALF = 30
PAIRS = [(p, q) for p in range(4) for q in range(p, 4)]
PAIR_ROWS = 8 * len(PAIRS)
RIGHT_ROWS = 16
BAND_ROWS = 4 * len(PAIRS)
ROWS = 48
STAT_ROWS = 24
F32 = jnp.float32
BF16 = jnp.bfloat16
NT = (((1,), (1,)), ((), ()))
SPLINE = [
    [1 / 6, 0.0, 0.0, 0.0],
    [4 / 6, 12 / 6, 6 / 6, 1 / 6],
    [1 / 6, 6 / 6, 12 / 6, 4 / 6],
    [0.0, 0.0, 0.0, 1 / 6],
]


def iota(shape, dim):
    return lax.broadcasted_iota(jnp.int32, shape, dim)


def split2(values):
    high = values.astype(BF16)
    return high, (values - high.astype(F32)).astype(BF16)


def split3(values):
    high = values.astype(BF16)
    rest = values - high.astype(F32)
    mid = rest.astype(BF16)
    return high, mid, (rest - mid.astype(F32)).astype(BF16)


def spline_weights(phase):
    square = phase * phase
    cube = square * phase
    rest = 1.0 - phase
    return [
        rest * rest * rest * (1.0 / 6.0),
        (3.0 * cube - 6.0 * square + 4.0) * (1.0 / 6.0),
        (-3.0 * cube + 3.0 * square + 3.0 * phase + 1.0) * (1.0 / 6.0),
        cube * (1.0 / 6.0),
    ]


def params(megabytes):
    return pltpu.CompilerParams(vmem_limit_bytes=megabytes * 1024 * 1024)


VMEM = pl.BlockSpec(memory_space=pltpu.VMEM)
SMEM = pl.BlockSpec(memory_space=pltpu.SMEM)
HBM = pl.BlockSpec(memory_space=pltpu.HBM)


def stats_kernel(
    design_in, weight_in, resid_in, source_ref, out_ref, design_ref, weight_ref, resid_ref, sums_ref, sems
):
    chunks = 4
    size = BLK_DEV // chunks
    copies = []
    for chunk in range(chunks):
        at = pl.ds(chunk * size, size)
        copies.append(
            [
                pltpu.make_async_copy(design_in.at[:, at], design_ref.at[:, at], sems.at[chunk, 0]),
                pltpu.make_async_copy(weight_in.at[at], weight_ref.at[at], sems.at[chunk, 1]),
                pltpu.make_async_copy(resid_in.at[at], resid_ref.at[at], sems.at[chunk, 2]),
            ]
        )
        for copy in copies[chunk]:
            copy.start()
    rows = 32
    lane = iota((rows, OBS), 1)
    for chunk in range(chunks):
        for copy in copies[chunk]:
            copy.wait()
        for group in range(size // rows):
            at = pl.ds(chunk * size + group * rows, rows)
            weight = weight_ref[at, :]
            design = [design_ref[p, at, :] for p in range(5)]
            resid = resid_ref[at, :]
            weighted = [weight * design[p] for p in range(5)]
            packed = jnp.zeros((rows, OBS), F32)
            slot = 0
            for p in range(5):
                for q in range(p + 1):
                    total = jnp.sum(weighted[p] * design[q], axis=1, keepdims=True)
                    packed = jnp.where(lane == slot, total, packed)
                    slot += 1
            for p in range(5):
                total = jnp.sum(weighted[p] * resid, axis=1, keepdims=True)
                packed = jnp.where(lane == slot, total, packed)
                slot += 1
            sums_ref[at, :] = packed
    local = jnp.bitwise_and(source_ref[...], SRC_DEV - 1)
    hot = (iota((SRC_DEV, BLK_DEV), 0) == local).astype(F32).astype(BF16)
    total = jnp.zeros((SRC_DEV, OBS), F32)
    for piece in split3(sums_ref[...]):
        total = total + jnp.dot(hot, piece, preferred_element_type=F32)
    out_ref[...] = total.T[:STAT_ROWS]


def source_sums(design, weight, resid, source_row):
    return pl.pallas_call(
        stats_kernel,
        out_shape=jax.ShapeDtypeStruct((STAT_ROWS, SRC_DEV), F32),
        in_specs=[HBM] * 3 + [VMEM],
        out_specs=VMEM,
        scratch_shapes=[
            pltpu.VMEM((5, BLK_DEV, OBS), F32),
            pltpu.VMEM((BLK_DEV, OBS), F32),
            pltpu.VMEM((BLK_DEV, OBS), F32),
            pltpu.VMEM((BLK_DEV, OBS), F32),
            pltpu.SemaphoreType.DMA((4, 3)),
        ],
        compiler_params=params(56),
        name="source_sums",
    )(design, weight, resid, source_row)


def roll(values, amount, axis):
    size = values.shape[axis]
    return pltpu.roll(values, amount % size, axis) if amount % size else values


def convolved(first, second):
    out = [0.0] * 7
    for i in range(4):
        for j in range(4):
            out[i + j] += SPLINE[first][i] * SPLINE[second][j]
    return out


def fold_bands(term_ref, out_ref):
    low_terms = [term_ref[pl.ds(k, 8, stride=8), :] for k in range(7)]
    high_terms = [term_ref[pl.ds(64 + k, 2, stride=8), :] for k in range(7)]
    for spacing in range(4):
        low = high = None
        for first in range(4 - spacing):
            low_slot = high_slot = None
            for k, weight in enumerate(convolved(first, first + spacing)):
                if weight != 0.0:
                    low_slot = plus(low_slot, weight * low_terms[k])
                    high_slot = plus(high_slot, weight * high_terms[k])
            low = plus(low, roll(low_slot, first, 1))
            high = plus(high, roll(high_slot, first, 1))
        out_ref[spacing * 10 : spacing * 10 + 8, :] = low
        out_ref[spacing * 10 + 8 : spacing * 10 + 10, :] = high


def plus(total, value):
    return value if total is None else total + value


def column_window(window_ref, block):
    window = window_ref[block]
    return lax.shift_right_logical(window, 4) * 2 + jnp.bitwise_and(window, 1)


def normals_kernel(
    comp_ref,
    phase_ref,
    knot_ref,
    weight_ref,
    list_ref,
    count_ref,
    window_ref,
    out_ref,
    watt_ref,
    poly_ref,
    pair_ref,
    total_ref,
    joined_ref,
):
    named = jnp.zeros((16, BLK_DEV // 8), F32)
    capacity = list_ref.shape[1]
    slot = iota((1, capacity), 1)
    for owner in range(N_SRC):
        entry = jnp.where(slot < count_ref[owner], list_ref[owner : owner + 1, :], -1)
        group_hot = iota((BLK_DEV // 8, capacity), 0) == lax.shift_right_arithmetic(entry, 3)
        place_hot = iota((16, capacity), 0) == jnp.where(entry < 0, -1, jnp.bitwise_and(entry, 7))
        named = named + lax.dot_general(
            place_hot.astype(F32).astype(BF16),
            group_hot.astype(F32).astype(BF16),
            NT,
            preferred_element_type=F32,
        )
    named = jnp.concatenate([named[:8], jnp.zeros((8, OBS - BLK_DEV // 8), F32)], axis=1)

    def prepare(group, carry):
        at = pl.ds(pl.multiple_of(group * 8, 8), 8)
        phase = phase_ref[at, :]
        rest = 1.0 - phase
        up = [None, phase, phase * phase, None]
        down = [None, rest, rest * rest, None]
        up[3] = up[2] * phase
        down[3] = down[2] * rest
        poly = [
            down[3] * down[3],
            phase * (down[3] * down[2]),
            up[2] * (down[2] * down[2]),
            up[3] * down[3],
            (up[2] * up[2]) * down[2],
            (up[3] * up[2]) * rest,
            up[3] * up[3],
            jnp.zeros_like(phase),
        ]
        for k in range(8):
            poly_ref[pl.ds(group * 64 + k, 8, stride=8), :] = poly[k]
        times = jnp.take_along_axis(named, jnp.full((8, OBS), group, jnp.int32), axis=1)
        weight = weight_ref[at, :] * times
        watt_ref[at, :] = weight
        comps = [comp_ref[pl.ds(group * 32 + p, 8, stride=4), :] for p in range(4)]
        weighted = [weight * comps[p] for p in range(4)]
        for i, (p, q) in enumerate(PAIRS):
            pair_ref[i, at, :] = weighted[p] * comps[q]
        return carry

    lax.fori_loop(0, BLK_DEV // 8, prepare, 0, unroll=8)
    total_ref[...] = jnp.zeros_like(total_ref)
    knot_iota = iota((KNOTS, OBS), 0)
    unrolled = 64

    def one_group(group, carry):
        for i in range(unrolled):
            block = group * unrolled + i
            poly = poly_ref[pl.ds(pl.multiple_of(block * 8, 8), 8), :]
            terms = jnp.concatenate(
                [poly * pair_ref[n, pl.ds(block, 1), :] for n in range(len(PAIRS))], axis=0
            )
            high, low = split2(terms)
            hot = (knot_iota == knot_ref[pl.ds(block, 1), :]).astype(F32).astype(BF16)
            summed = lax.dot_general(
                jnp.concatenate([high, low], axis=1),
                jnp.concatenate([hot, hot], axis=1),
                NT,
                preferred_element_type=F32,
            )
            at = column_window(window_ref, block)
            total_ref[at] = total_ref[at] + summed
        return carry

    lax.fori_loop(0, BLK_DEV // unrolled, one_group, 0)
    for owner in range(N_SRC):
        joined_ref[owner, :, :] = jnp.concatenate(
            [total_ref[2 * owner], total_ref[2 * owner + 1]], axis=1
        )
    for owner in range(N_SRC):
        fold_bands(joined_ref.at[owner], out_ref.at[owner])


def normal_sums(comps, phase, knots, weight, lists, counts, window):
    return pl.pallas_call(
        normals_kernel,
        out_shape=(
            jax.ShapeDtypeStruct((N_SRC, BAND_ROWS, OBS), F32),
            jax.ShapeDtypeStruct((BLK_DEV, OBS), F32),
        ),
        in_specs=[VMEM] * 5 + [SMEM] * 2,
        out_specs=(VMEM, VMEM),
        scratch_shapes=[
            pltpu.VMEM((BLK_DEV * 8, OBS), F32),
            pltpu.VMEM((len(PAIRS), BLK_DEV, OBS), F32),
            pltpu.VMEM((N_COL, PAIR_ROWS, KNOTS), F32),
            pltpu.VMEM((N_SRC, PAIR_ROWS, OBS), F32),
        ],
        compiler_params=params(32),
        cost_estimate=pl.CostEstimate(flops=3_000_000_000, bytes_accessed=4_000_000, transcendentals=0),
        name="normal_sums",
    )(comps, phase, knots, weight, lists, counts, window)


def solve_five(totals):
    def entry_at(across, within):
        row = across * (across + 1) // 2 + within
        return totals[row : row + 1, :]

    factor = {}
    inverse = {}
    for across in range(5):
        for within in range(across + 1):
            entry = entry_at(across, within)
            if across == within:
                entry = entry + 1.0
            for before in range(within):
                entry = entry - factor[across, before] * factor[within, before]
            if across == within:
                inverse[across] = 1.0 / jnp.sqrt(entry)
            else:
                factor[across, within] = entry * inverse[within]
    forward = []
    for across in range(5):
        entry = totals[15 + across : 16 + across, :]
        for before in range(across):
            entry = entry - factor[across, before] * forward[before]
        forward.append(entry * inverse[across])
    backward = [None] * 5
    for across in range(4, -1, -1):
        entry = forward[across]
        for later in range(across + 1, 5):
            entry = entry - factor[later, across] * backward[later]
        backward[across] = entry * inverse[across]
    return backward


def rights_kernel(
    own_ref,
    near_ref,
    far_ref,
    cross_ref,
    design_ref,
    resid_ref,
    watt_ref,
    comp_ref,
    phase_ref,
    knot_ref,
    source_ref,
    window_ref,
    bands_ref,
    step_ref,
    first_ref,
    sums_ref,
    column_ref,
    term_ref,
    total_ref,
):
    totals = (own_ref[...] + near_ref[...]) + (far_ref[...] + cross_ref[...])
    step = solve_five(totals)
    for p in range(5):
        step_ref[p : p + 1, :] = step[p]
    stacked = jnp.concatenate(step + [jnp.zeros((3, SRC_DEV), F32)], axis=0)
    pieces = jnp.concatenate(list(split3(stacked)) + [jnp.zeros((8, SRC_DEV), BF16)], axis=0)
    local = jnp.bitwise_and(source_ref[...], SRC_DEV - 1)
    hot = (iota((SRC_DEV, BLK_DEV), 0) == local).astype(F32).astype(BF16)
    picked = jnp.dot(pieces, hot, preferred_element_type=F32)
    picked = picked[:8] + picked[8:16] + picked[16:24]
    column_ref[...] = jnp.concatenate([picked, jnp.zeros((OBS - 8, BLK_DEV), F32)], axis=0).T

    def prepare(group, carry):
        at = pl.ds(pl.multiple_of(group * 8, 8), 8)
        columns = column_ref[at, :]
        fitted = jnp.zeros((8, OBS), F32)
        for p in range(5):
            fitted = fitted + design_ref[p, at, :] * columns[:, p : p + 1]
        first = resid_ref[at, :] - fitted
        first_ref[at, :] = first
        weighted = watt_ref[at, :] * first
        spline = spline_weights(phase_ref[at, :])
        comps = [comp_ref[pl.ds(group * 32 + p, 8, stride=4), :] for p in range(4)]
        for m in range(4):
            scaled = weighted * spline[m]
            for p in range(4):
                term_ref[pl.ds(group * 128 + 4 * m + p, 8, stride=16), :] = scaled * comps[p]
        return carry

    lax.fori_loop(0, BLK_DEV // 8, prepare, 0, unroll=8)
    total_ref[...] = jnp.zeros_like(total_ref)
    knot_iota = iota((KNOTS, OBS), 0)
    unrolled = 64

    def one_group(group, carry):
        for i in range(unrolled):
            block = group * unrolled + i
            terms = term_ref[pl.ds(pl.multiple_of(block * 16, 16), 16), :]
            high, low = split2(terms)
            hot = (knot_iota == knot_ref[pl.ds(block, 1), :]).astype(F32).astype(BF16)
            summed = lax.dot_general(
                jnp.concatenate([high, low], axis=1),
                jnp.concatenate([hot, hot], axis=1),
                NT,
                preferred_element_type=F32,
            )
            at = column_window(window_ref, block)
            total_ref[at] = total_ref[at] + summed
        return carry

    lax.fori_loop(0, BLK_DEV // unrolled, one_group, 0)
    for owner in range(N_SRC):
        joined = jnp.concatenate([total_ref[2 * owner], total_ref[2 * owner + 1]], axis=1)
        right = joined[:4]
        for first in range(1, 4):
            right = right + roll(joined[4 * first : 4 * first + 4], first, 1)
        sums_ref[owner, :BAND_ROWS, :] = bands_ref[owner]
        sums_ref[owner, BAND_ROWS:, :] = jnp.concatenate([right, jnp.zeros((4, OBS), F32)], axis=0)


def right_sums(parts, design, resid, watt, comps, phase, knots, source_row, window, sums):
    return pl.pallas_call(
        rights_kernel,
        out_shape=(
            jax.ShapeDtypeStruct((5, SRC_DEV), F32),
            jax.ShapeDtypeStruct((BLK_DEV, OBS), F32),
            jax.ShapeDtypeStruct((N_SRC, ROWS, OBS), F32),
        ),
        in_specs=[VMEM] * 11 + [SMEM, VMEM],
        out_specs=(VMEM, VMEM, VMEM),
        scratch_shapes=[
            pltpu.VMEM((BLK_DEV, OBS), F32),
            pltpu.VMEM((BLK_DEV * 16, OBS), F32),
            pltpu.VMEM((N_COL, RIGHT_ROWS, KNOTS), F32),
        ],
        compiler_params=params(32),
        name="right_sums",
    )(*parts, design, resid, watt, comps, phase, knots, source_row, window, sums)


def solve_kernel(prior, got_ref, out_ref, work_ref):
    total = got_ref[0]
    for other in range(1, N_SRC):
        total = total + got_ref[other]
    lane8 = iota((8, OBS), 1)
    sublane8 = iota((8, OBS), 0)
    index = {}
    for i, (p, q) in enumerate(PAIRS):
        index[p, q] = index[q, p] = i
    bands = []
    for spacing in range(4):
        rows = [total[spacing * 10 + i : spacing * 10 + i + 1] for i in range(10)]
        if spacing == 0:
            rows = [row + prior if PAIRS[i][0] == PAIRS[i][1] else row for i, row in enumerate(rows)]
        full = [rows[index[p, q]] for p in range(4) for q in range(4)]
        bands.append([jnp.concatenate(full[:8], axis=0), jnp.concatenate(full[8:], axis=0)])
    right = total[BAND_ROWS : BAND_ROWS + 4]
    right = jnp.concatenate([right, right], axis=0)

    place = jnp.bitwise_and(lane8, 31)
    window_at = jnp.bitwise_and(lane8, 64)
    is_down = jnp.bitwise_and(lane8, 32) != 0

    def arranged(values, spacing, base):
        step = place + base
        up_index = jnp.minimum(window_at + step, OBS - 1)
        down_index = jnp.maximum(window_at + KNOTS - 1 - step, 0)
        up = jnp.take_along_axis(roll(values, spacing, 1), up_index, axis=1)
        down = jnp.take_along_axis(values, down_index, axis=1)
        down = jnp.where(step - spacing >= HALF, 0.0, down)
        return jnp.where(is_down, down, up)

    def entering(base):
        return [arranged(bands[d][h], d, base) for d in range(4) for h in range(2)] + [
            arranged(right, 0, base)
        ]

    stream, tail = entering(0), entering(32)

    lower = sublane8 < 4

    def insert(front, target, pieces, slot, present):
        def part(d, p, half):
            values = pieces[2 * d + p // 2]
            return values if p % 2 == half else roll(values, 4, 0)

        for d in range(1, present + 1):
            other = (slot - d) % 4
            for q in range(4):
                old = front[other * 4 + q]
                fresh = part(d, q, slot % 2)
                keep = lower if slot % 2 == 1 else jnp.logical_not(lower)
                old[slot // 2] = jnp.where(keep, old[slot // 2], fresh)
        for p in range(4):
            halves = []
            for h in range(2):
                both = []
                for spot in range(2):
                    d = (slot - (2 * h + spot)) % 4
                    both.append(part(d, p, spot) if d <= present else jnp.zeros((8, OBS), F32))
                halves.append(jnp.where(lower, both[0], both[1]))
            front[slot * 4 + p] = halves
        keep = lower if slot % 2 == 1 else jnp.logical_not(lower)
        target[slot // 2] = jnp.where(keep, target[slot // 2], pieces[8])

    def eliminate(front, target, slot, gone):
        scale = None
        for p in range(4):
            row = slot * 4 + p
            half, at = row // 8, row % 8
            column = front[row]
            inverse = 1.0 / column[half][at : at + 1, :]
            scale = inverse if scale is None else jnp.where(sublane8 == at, inverse, scale)
            factor = [column[h] * inverse for h in range(2)]
            factor[half] = jnp.where(sublane8 == at, 0.0, factor[half])
            gone = gone | {row}
            for c in [c for c in range(16) if c not in gone] + [16]:
                values = target if c == 16 else front[c]
                pivot = values[half][at : at + 1, :]
                for h in range(2):
                    values[h] = values[h] - factor[h] * pivot
        return gone, scale

    def save(front, target, slot, step, scale):
        for r in range(1, 4):
            for q in range(4):
                work_ref[step * 13 + (r - 1) * 4 + q] = (
                    front[(slot + r) % 4 * 4 + q][slot // 2] * scale
                )
        work_ref[step * 13 + 12] = target[slot // 2] * scale

    zero = jnp.zeros((8, OBS), F32)
    front = [[zero, zero] for _ in range(16)]
    target = [zero, zero]
    for step in range(4):
        insert(front, target, [roll(values, -step, 1) for values in stream], step, step)
    for step in range(HALF):
        slot = step % 4
        unused, scale = eliminate(front, target, slot, frozenset())
        save(front, target, slot, step, scale)
        source, shift = (stream, step + 4) if step < 28 else (tail, step - 28)
        insert(front, target, [roll(values, -shift, 1) for values in source], slot, 3)

    mirror = jnp.bitwise_xor(lane8, 32)

    def mirrored(values):
        return jnp.take_along_axis(roll(values, 4, 0), mirror, axis=1)

    front = [
        [front[a * 4 + p][h] + mirrored(front[(3 - a) * 4 + p][1 - h]) for h in range(2)]
        for a in range(4)
        for p in range(4)
    ]
    target = [target[h] + mirrored(target[1 - h]) for h in range(2)]
    gone = frozenset()
    scales = {}
    for slot in (2, 3, 0, 1):
        gone, scales[slot] = eliminate(front, target, slot, gone)
    target = [
        target[h] * jnp.where(lower, scales[2 * h], scales[2 * h + 1]) for h in range(2)
    ]

    first_lane = place == 0
    placed = []

    def emit(answer, slot, step):
        values = answer[slot // 2]
        values = values if slot % 2 == 0 else roll(values, 4, 0)
        placed.append(roll(jnp.where(first_lane, values, 0.0), step, 1))

    def back(answer, slot, step):
        half = slot // 2
        parts = [work_ref[step * 13 + 12]]
        for r in (3, 2, 1):
            other = (slot + r) % 4
            terms = []
            for q in range(4):
                at = other % 2 * 4 + q
                terms.append(
                    work_ref[step * 13 + (r - 1) * 4 + q] * answer[other // 2][at : at + 1, :]
                )
            parts.append((terms[0] + terms[1]) + (terms[2] + terms[3]))
        fresh = ((parts[0] - parts[1]) - parts[2]) - parts[3]
        keep = lower if slot % 2 == 1 else jnp.logical_not(lower)
        answer[half] = jnp.where(keep, answer[half], fresh)

    answer = list(target)
    emit(answer, 3, 31)
    emit(answer, 2, 30)
    for step in range(HALF - 1, -1, -1):
        back(answer, step % 4, step)
        emit(answer, step % 4, step)
    while len(placed) > 1:
        placed = [placed[i] + placed[i + 1] for i in range(0, len(placed), 2)]
    result = placed[0]
    knot = jnp.bitwise_and(lane8, KNOTS - 1)
    from_lane = jnp.where(knot < 32, lane8, window_at + 32 + KNOTS - 1 - knot)
    panel = jnp.take_along_axis(result, from_lane, axis=1)
    for owner in range(N_SRC):
        out_ref[owner] = panel


def solve_panels(got, prior):
    def body(*refs):
        solve_kernel(prior, *refs)

    return pl.pallas_call(
        body,
        out_shape=jax.ShapeDtypeStruct((N_SRC, 8, OBS), F32),
        in_specs=[VMEM],
        out_specs=VMEM,
        scratch_shapes=[pltpu.VMEM((HALF * 13, 8, OBS), F32)],
        compiler_params=params(16),
        name="solve_panels",
    )(got)


def final_kernel(panel_ref, comp_ref, phase_ref, knot_ref, first_ref, window_ref, out_ref, table_ref):
    for owner in range(N_SRC):
        tile = panel_ref[owner]
        table_ref[owner * 16 : owner * 16 + 8, :] = tile
        table_ref[owner * 16 + 8 : owner * 16 + 16, :] = roll(tile, 64, 1)

    def one_group(group, carry):
        at = pl.ds(pl.multiple_of(group * 8, 8), 8)
        knots = knot_ref[at, :]
        spline = spline_weights(phase_ref[at, :])
        starts = [column_window(window_ref, group * 8 + i) * 8 for i in range(8)]
        correction = [jnp.zeros((8, OBS), F32) for _ in range(4)]
        for p in range(4):
            table = jnp.concatenate([table_ref[pl.ds(start + p, 1), :] for start in starts], axis=0)
            comps = comp_ref[pl.ds(group * 32 + p, 8, stride=4), :]
            for m in range(4):
                correction[m] = correction[m] + comps * jnp.take_along_axis(table, knots + m, axis=1)
        total = spline[0] * correction[0]
        for m in range(1, 4):
            total = total + spline[m] * correction[m]
        out_ref[at, :] = first_ref[at, :] - total
        return carry

    lax.fori_loop(0, BLK_DEV // 8, one_group, 0, unroll=16)


def final_residual(panels, comps, phase, knots, first, window):
    return pl.pallas_call(
        final_kernel,
        out_shape=jax.ShapeDtypeStruct((BLK_DEV, OBS), F32),
        in_specs=[VMEM] * 5 + [SMEM],
        out_specs=VMEM,
        scratch_shapes=[pltpu.VMEM((N_COL * 8, OBS), F32)],
        compiler_params=params(16),
        name="final_residual",
    )(panels, comps, phase, knots, first, window)


def shards(
    src_design,
    att_comp,
    spline_phase,
    knot_offset,
    obs_weight,
    residual,
    block_source,
    block_window,
    send_list,
    send_count,
):
    n_win = lax.axis_size("win")
    design = src_design.transpose(1, 0, 2)
    comps = att_comp.reshape(BLK_DEV * 4, OBS)
    source_row = block_source.reshape(1, BLK_DEV)
    obs_src = OBS * BLK_DEV * n_win // SRC_DEV
    obs_win = OBS * BLK_DEV // WIN_SUB
    prior = 0.005 * obs_win / obs_src

    def swap(values, bit):
        return lax.ppermute(values, "win", [(i, i ^ bit) for i in range(n_win)])

    stats = source_sums(design, obs_weight, residual, source_row)
    stats = stats + swap(stats, 1)
    parts = (stats, swap(stats, 2), swap(stats, 4), swap(stats, 6))
    sums, watt = normal_sums(
        comps, spline_phase, knot_offset, obs_weight, send_list, send_count, block_window
    )
    source_step, first, sums = right_sums(
        parts,
        design,
        residual,
        watt,
        comps,
        spline_phase,
        knot_offset,
        source_row,
        block_window,
        sums,
    )
    got = lax.all_to_all(sums, "src", split_axis=0, concat_axis=0, tiled=True)
    own_panels = solve_panels(got, prior)
    panels = lax.all_to_all(own_panels, "src", split_axis=0, concat_axis=0, tiled=True)
    attitude_step = (
        own_panels[0, :4].reshape(4, WIN_SUB, KNOTS).transpose(1, 2, 0).reshape(WIN_SUB, KNOTS * 4)
    )
    last = final_residual(panels, comps, spline_phase, knot_offset, first, block_window)
    return (source_step, attitude_step, last)


def solution(mesh):
    return jax.shard_map(
        shards,
        mesh=mesh,
        in_specs=(
            P(("src", "win"), None, None),
            P(("src", "win"), None, None),
            P(("src", "win"), None),
            P(("src", "win"), None),
            P(("src", "win"), None),
            P(("src", "win"), None),
            P(("src", "win")),
            P(("src", "win")),
            P(("src", "win"), None),
            P(("src", "win")),
        ),
        out_specs=(P(None, "src"), P(("src", "win"), None), P(("src", "win"), None)),
        check_vma=False,
    )
```

```python
import jax
import jax.numpy as jnp
from jax import lax
from jax.experimental import pallas as pl
from jax.experimental.pallas import tpu as pltpu
from jax.sharding import PartitionSpec as P

OBS = 128
KNOTS = 64
WIN_SUB = 2
BLK_DEV = 512
SRC_DEV = 256
N_SRC = 16
N_COL = N_SRC * WIN_SUB
HALF = 30
PAIRS = [(p, q) for p in range(4) for q in range(p, 4)]
PAIR_ROWS = 8 * len(PAIRS)
RIGHT_ROWS = 16
BAND_ROWS = 4 * len(PAIRS)
ROWS = 48
STAT_ROWS = 24
CODES = 384
N_PAIR = 272
NO_BLOCK = 512
F32 = jnp.float32
BF16 = jnp.bfloat16
NT = (((1,), (1,)), ((), ()))
SPLINE = [
    [1 / 6, 0.0, 0.0, 0.0],
    [4 / 6, 12 / 6, 6 / 6, 1 / 6],
    [1 / 6, 6 / 6, 12 / 6, 4 / 6],
    [0.0, 0.0, 0.0, 1 / 6],
]


def iota(shape, dim):
    return lax.broadcasted_iota(jnp.int32, shape, dim)


def split2(values):
    high = values.astype(BF16)
    return high, (values - high.astype(F32)).astype(BF16)


def split3(values):
    high = values.astype(BF16)
    rest = values - high.astype(F32)
    mid = rest.astype(BF16)
    return high, mid, (rest - mid.astype(F32)).astype(BF16)


def spline_weights(phase):
    square = phase * phase
    cube = square * phase
    rest = 1.0 - phase
    return [
        rest * rest * rest * (1.0 / 6.0),
        (3.0 * cube - 6.0 * square + 4.0) * (1.0 / 6.0),
        (-3.0 * cube + 3.0 * square + 3.0 * phase + 1.0) * (1.0 / 6.0),
        cube * (1.0 / 6.0),
    ]


def params(megabytes):
    return pltpu.CompilerParams(vmem_limit_bytes=int(megabytes * 1024 * 1024))


VMEM = pl.BlockSpec(memory_space=pltpu.VMEM)
SMEM = pl.BlockSpec(memory_space=pltpu.SMEM)
HBM = pl.BlockSpec(memory_space=pltpu.HBM)


def column_window(window_ref, block):
    window = window_ref[block]
    return lax.shift_right_logical(window, 4) * 2 + jnp.bitwise_and(window, 1)


def stats_kernel(
    design_in, weight_in, resid_in, source_ref, out_ref, design_ref, weight_ref, resid_ref, sums_ref, sems
):
    chunks = 4
    size = BLK_DEV // chunks
    copies = []
    for chunk in range(chunks):
        at = pl.ds(chunk * size, size)
        copies.append(
            [
                pltpu.make_async_copy(design_in.at[:, at], design_ref.at[:, at], sems.at[chunk, 0]),
                pltpu.make_async_copy(weight_in.at[at], weight_ref.at[at], sems.at[chunk, 1]),
                pltpu.make_async_copy(resid_in.at[at], resid_ref.at[at], sems.at[chunk, 2]),
            ]
        )
        for copy in copies[chunk]:
            copy.start()
    rows = 32
    lane = iota((rows, OBS), 1)
    for chunk in range(chunks):
        for copy in copies[chunk]:
            copy.wait()
        for group in range(size // rows):
            at = pl.ds(chunk * size + group * rows, rows)
            weight = weight_ref[at, :]
            design = [design_ref[p, at, :] for p in range(5)]
            resid = resid_ref[at, :]
            weighted = [weight * design[p] for p in range(5)]
            packed = jnp.zeros((rows, OBS), F32)
            slot = 0
            for p in range(5):
                for q in range(p + 1):
                    total = jnp.sum(weighted[p] * design[q], axis=1, keepdims=True)
                    packed = jnp.where(lane == slot, total, packed)
                    slot += 1
            for p in range(5):
                total = jnp.sum(weighted[p] * resid, axis=1, keepdims=True)
                packed = jnp.where(lane == slot, total, packed)
                slot += 1
            sums_ref[at, :] = packed
    local = jnp.bitwise_and(source_ref[...], SRC_DEV - 1)
    hot = (iota((SRC_DEV, BLK_DEV), 0) == local).astype(F32).astype(BF16)
    total = jnp.zeros((SRC_DEV, OBS), F32)
    for piece in split3(sums_ref[...]):
        total = total + jnp.dot(hot, piece, preferred_element_type=F32)
    out_ref[...] = total.T[:STAT_ROWS]


def source_sums(design, weight, resid, source_row):
    return pl.pallas_call(
        stats_kernel,
        out_shape=pltpu.VMEM((STAT_ROWS, SRC_DEV), F32),
        in_specs=[HBM] * 3 + [VMEM],
        out_specs=VMEM,
        scratch_shapes=[
            pltpu.VMEM((5, BLK_DEV, OBS), F32),
            pltpu.VMEM((BLK_DEV, OBS), F32),
            pltpu.VMEM((BLK_DEV, OBS), F32),
            pltpu.VMEM((BLK_DEV, OBS), F32),
            pltpu.SemaphoreType.DMA((4, 3)),
        ],
        compiler_params=params(54),
        name="source_sums",
    )(*(pltpu.with_memory_space_constraint(x, pltpu.HBM) for x in (design, weight, resid)), source_row)


def roll(values, amount, axis):
    size = values.shape[axis]
    return pltpu.roll(values, amount % size, axis) if amount % size else values


def convolved(first, second):
    out = [0.0] * 7
    for i in range(4):
        for j in range(4):
            out[i + j] += SPLINE[first][i] * SPLINE[second][j]
    return out


def fold_bands(term_ref, out_ref):
    low_terms = [term_ref[pl.ds(k, 8, stride=8), :] for k in range(7)]
    high_terms = [term_ref[pl.ds(64 + k, 2, stride=8), :] for k in range(7)]
    for spacing in range(4):
        low = high = None
        for first in range(4 - spacing):
            low_slot = high_slot = None
            for k, weight in enumerate(convolved(first, first + spacing)):
                if weight != 0.0:
                    low_slot = plus(low_slot, weight * low_terms[k])
                    high_slot = plus(high_slot, weight * high_terms[k])
            low = plus(low, roll(low_slot, first, 1))
            high = plus(high, roll(high_slot, first, 1))
        out_ref[spacing * 10 : spacing * 10 + 8, :] = low
        out_ref[spacing * 10 + 8 : spacing * 10 + 10, :] = high


def plus(total, value):
    return value if total is None else total + value


def pair_members(code_ref, pair):
    code = code_ref[0, pair]
    blocks = []
    for shift in (0, 10):
        block = jnp.bitwise_and(lax.shift_right_logical(code, shift), 1023)
        blocks.append((jnp.minimum(block, BLK_DEV - 1), jnp.bitwise_and(block, NO_BLOCK)))
    return lax.shift_right_logical(code, 20), blocks


def pair_codes(window):
    column = lax.shift_right_logical(window, 4) * 2 + jnp.bitwise_and(window, 1)
    hot = (iota((N_COL, BLK_DEV), 0) == column).astype(F32)
    before = (iota((OBS, OBS), 0) < iota((OBS, OBS), 1)).astype(F32).astype(BF16)
    count = jnp.zeros((N_COL, 1), F32)
    ranks = []
    for start in range(0, BLK_DEV, OBS):
        part = hot[:, start : start + OBS]
        seen = jnp.dot(part.astype(BF16), before, preferred_element_type=F32) + count
        ranks.append(jnp.sum(part * seen, axis=0, keepdims=True))
        count = count + jnp.sum(part, axis=1, keepdims=True)
    rank = jnp.concatenate(ranks, axis=1).astype(jnp.int32)
    pairs = lax.shift_right_logical(count.astype(jnp.int32) + 1, 1).astype(F32)
    below = (iota((N_COL, N_COL), 1) < iota((N_COL, N_COL), 0)).astype(F32).astype(BF16)
    spread = jnp.broadcast_to(pairs, (N_COL, OBS)).astype(BF16)
    start = jnp.dot(below, spread, preferred_element_type=F32)[:, :1]
    pair = jnp.sum(hot * start, axis=0, keepdims=True).astype(jnp.int32)
    pair = pair + lax.shift_right_logical(rank, 1)
    second = jnp.bitwise_and(rank, 1)
    missing = NO_BLOCK - iota((1, BLK_DEV), 1)
    high, low = lax.shift_right_logical(missing, 4), jnp.bitwise_and(missing, 15)
    first = 1 - second
    rows = [first * high, first * low, second * high, second * low, first * column]
    rows = jnp.concatenate([row.astype(F32) for row in rows] + [jnp.zeros((11, BLK_DEV), F32)], axis=0)
    target = (iota((CODES, BLK_DEV), 0) == pair).astype(F32).astype(BF16)
    found = lax.dot_general(rows.astype(BF16), target, NT, preferred_element_type=F32)
    found = found.astype(jnp.int32)
    left = NO_BLOCK - found[0:1] * 16 - found[1:2]
    right = NO_BLOCK - found[2:3] * 16 - found[3:4]
    return left + right * 1024 + found[4:5] * (1 << 20)


def knots_hot(knot_ref, block, offset):
    hot = iota((KNOTS, OBS), 0) == knot_ref[pl.ds(block, 1), :] + offset
    return hot.astype(F32).astype(BF16)


def normals_kernel(
    comp_ref,
    phase_ref,
    knot_ref,
    weight_ref,
    list_ref,
    window_row_ref,
    count_ref,
    window_ref,
    out_ref,
    watt_ref,
    code_ref,
    poly_ref,
    pair_ref,
    total_ref,
    joined_ref,
):
    code_ref[...] = pair_codes(window_row_ref[...])
    named = jnp.zeros((16, BLK_DEV // 8), F32)
    capacity = list_ref.shape[1]
    slot = iota((1, capacity), 1)
    for owner in range(N_SRC):
        entry = jnp.where(slot < count_ref[owner], list_ref[owner : owner + 1, :], -1)
        group_hot = iota((BLK_DEV // 8, capacity), 0) == lax.shift_right_arithmetic(entry, 3)
        place_hot = iota((16, capacity), 0) == jnp.where(entry < 0, -1, jnp.bitwise_and(entry, 7))
        named = named + lax.dot_general(
            place_hot.astype(F32).astype(BF16),
            group_hot.astype(F32).astype(BF16),
            NT,
            preferred_element_type=F32,
        )
    named = jnp.concatenate([named[:8], jnp.zeros((8, OBS - BLK_DEV // 8), F32)], axis=1)

    def prepare(group, carry):
        at = pl.ds(pl.multiple_of(group * 8, 8), 8)
        phase = phase_ref[at, :]
        rest = 1.0 - phase
        up = [None, phase, phase * phase, None]
        down = [None, rest, rest * rest, None]
        up[3] = up[2] * phase
        down[3] = down[2] * rest
        poly = [
            down[3] * down[3],
            phase * (down[3] * down[2]),
            up[2] * (down[2] * down[2]),
            up[3] * down[3],
            (up[2] * up[2]) * down[2],
            (up[3] * up[2]) * rest,
            up[3] * up[3],
            jnp.zeros_like(phase),
        ]
        for k in range(8):
            poly_ref[pl.ds(group * 64 + k, 8, stride=8), :] = poly[k]
        times = jnp.take_along_axis(named, jnp.full((8, OBS), group, jnp.int32), axis=1)
        weight = weight_ref[at, :] * times
        watt_ref[at, :] = weight
        comps = [comp_ref[pl.ds(group * 32 + p, 8, stride=4), :] for p in range(4)]
        weighted = [weight * comps[p] for p in range(4)]
        for i, (p, q) in enumerate(PAIRS):
            pair_ref[i, at, :] = weighted[p] * comps[q]
        return carry

    lax.fori_loop(0, BLK_DEV // 8, prepare, 0, unroll=16)
    total_ref[...] = jnp.zeros_like(total_ref)
    unrolled = 128

    def one_group(group, carry):
        for i in range(unrolled):
            block = group * unrolled + i
            poly = poly_ref[pl.ds(pl.multiple_of(block * 8, 8), 8), :]
            terms = jnp.concatenate(
                [poly * pair_ref[n, pl.ds(block, 1), :] for n in range(len(PAIRS))], axis=0
            )
            hot = knots_hot(knot_ref, block, 0)
            summed = lax.dot_general(
                jnp.concatenate(split2(terms), axis=1),
                jnp.concatenate([hot, hot], axis=1),
                NT,
                preferred_element_type=F32,
            )
            column = column_window(window_ref, block)
            total_ref[column] = total_ref[column] + summed
        return carry

    lax.fori_loop(0, BLK_DEV // unrolled, one_group, 0)
    for owner in range(N_SRC):
        joined_ref[owner, :, :] = jnp.concatenate(
            [total_ref[2 * owner], total_ref[2 * owner + 1]], axis=1
        )
    for owner in range(N_SRC):
        fold_bands(joined_ref.at[owner], out_ref.at[owner])


def normal_sums(comps, phase, knots, weight, lists, counts, window):
    return pl.pallas_call(
        normals_kernel,
        out_shape=(
            jax.ShapeDtypeStruct((N_SRC, BAND_ROWS, OBS), F32),
            jax.ShapeDtypeStruct((BLK_DEV, OBS), F32),
            jax.ShapeDtypeStruct((1, CODES), jnp.int32),
        ),
        in_specs=[VMEM] * 6 + [SMEM] * 2,
        out_specs=(VMEM, VMEM, VMEM),
        scratch_shapes=[
            pltpu.VMEM((BLK_DEV * 8, OBS), F32),
            pltpu.VMEM((len(PAIRS), BLK_DEV, OBS), F32),
            pltpu.VMEM((N_COL, PAIR_ROWS, KNOTS), F32),
            pltpu.VMEM((N_SRC, PAIR_ROWS, OBS), F32),
        ],
        compiler_params=params(32),
        cost_estimate=pl.CostEstimate(flops=3_000_000_000, bytes_accessed=4_000_000, transcendentals=0),
        name="normal_sums",
    )(comps, phase, knots, weight, lists, window.reshape(1, BLK_DEV), counts, window)


def solve_five(totals):
    def entry_at(across, within):
        row = across * (across + 1) // 2 + within
        return totals[row : row + 1, :]

    factor = {}
    inverse = {}
    for across in range(5):
        for within in range(across + 1):
            entry = entry_at(across, within)
            if across == within:
                entry = entry + 1.0
            for before in range(within):
                entry = entry - factor[across, before] * factor[within, before]
            if across == within:
                inverse[across] = 1.0 / jnp.sqrt(entry)
            else:
                factor[across, within] = entry * inverse[within]
    forward = []
    for across in range(5):
        entry = totals[15 + across : 16 + across, :]
        for before in range(across):
            entry = entry - factor[across, before] * forward[before]
        forward.append(entry * inverse[across])
    backward = [None] * 5
    for across in range(4, -1, -1):
        entry = forward[across]
        for later in range(across + 1, 5):
            entry = entry - factor[later, across] * backward[later]
        backward[across] = entry * inverse[across]
    return backward


def rights_kernel(
    own_ref,
    near_ref,
    far_ref,
    cross_ref,
    design_ref,
    resid_ref,
    watt_ref,
    comp_ref,
    phase_ref,
    knot_ref,
    source_ref,
    code_ref,
    bands_ref,
    step_ref,
    first_ref,
    sums_ref,
    column_ref,
    term_ref,
    total_ref,
):
    totals = (own_ref[...] + near_ref[...]) + (far_ref[...] + cross_ref[...])
    step = solve_five(totals)
    for p in range(5):
        step_ref[p : p + 1, :] = step[p]
    stacked = jnp.concatenate(step + [jnp.zeros((3, SRC_DEV), F32)], axis=0)
    pieces = jnp.concatenate(list(split3(stacked)) + [jnp.zeros((8, SRC_DEV), BF16)], axis=0)
    local = jnp.bitwise_and(source_ref[...], SRC_DEV - 1)
    hot = (iota((SRC_DEV, BLK_DEV), 0) == local).astype(F32).astype(BF16)
    picked = jnp.dot(pieces, hot, preferred_element_type=F32)
    picked = picked[:8] + picked[8:16] + picked[16:24]
    column_ref[...] = jnp.concatenate([picked, jnp.zeros((OBS - 8, BLK_DEV), F32)], axis=0).T

    def prepare(group, carry):
        at = pl.ds(pl.multiple_of(group * 8, 8), 8)
        columns = column_ref[at, :]
        fitted = jnp.zeros((8, OBS), F32)
        for p in range(5):
            fitted = fitted + design_ref[p, at, :] * columns[:, p : p + 1]
        first = resid_ref[at, :] - fitted
        first_ref[at, :] = first
        weighted = watt_ref[at, :] * first
        spline = spline_weights(phase_ref[at, :])
        comps = [comp_ref[pl.ds(group * 32 + p, 8, stride=4), :] for p in range(4)]
        for m in range(4):
            scaled = weighted * spline[m]
            for p in range(4):
                term_ref[pl.ds(group * 128 + 4 * m + p, 8, stride=16), :] = scaled * comps[p]
        return carry

    lax.fori_loop(0, BLK_DEV // 8, prepare, 0, unroll=16)
    total_ref[...] = jnp.zeros_like(total_ref)
    unrolled = 136

    def one_group(group, carry):
        for i in range(unrolled):
            at, blocks = pair_members(code_ref, group * unrolled + i)
            sides = []
            for block, offset in blocks:
                terms = term_ref[pl.ds(pl.multiple_of(block * 16, 16), 16), :]
                sides.append(
                    (jnp.concatenate(split2(terms), axis=0), knots_hot(knot_ref, block, offset))
                )
            summed = lax.dot_general(
                jnp.concatenate([sides[0][0], sides[1][0]], axis=1),
                jnp.concatenate([sides[0][1], sides[1][1]], axis=1),
                NT,
                preferred_element_type=F32,
            )
            total_ref[at] = total_ref[at] + (summed[:RIGHT_ROWS] + summed[RIGHT_ROWS:])
        return carry

    lax.fori_loop(0, N_PAIR // unrolled, one_group, 0)
    for owner in range(N_SRC):
        joined = jnp.concatenate([total_ref[2 * owner], total_ref[2 * owner + 1]], axis=1)
        right = joined[:4]
        for first in range(1, 4):
            right = right + roll(joined[4 * first : 4 * first + 4], first, 1)
        sums_ref[owner, :BAND_ROWS, :] = bands_ref[owner]
        sums_ref[owner, BAND_ROWS:, :] = jnp.concatenate([right, jnp.zeros((4, OBS), F32)], axis=0)


def right_sums(parts, design, resid, watt, comps, phase, knots, source_row, codes, sums):
    return pl.pallas_call(
        rights_kernel,
        out_shape=(
            jax.ShapeDtypeStruct((5, SRC_DEV), F32),
            jax.ShapeDtypeStruct((BLK_DEV, OBS), F32),
            jax.ShapeDtypeStruct((N_SRC, ROWS, OBS), F32),
        ),
        in_specs=[VMEM] * 11 + [SMEM, VMEM],
        out_specs=(VMEM, VMEM, VMEM),
        scratch_shapes=[
            pltpu.VMEM((BLK_DEV, OBS), F32),
            pltpu.VMEM((BLK_DEV * 16, OBS), F32),
            pltpu.VMEM((N_COL, RIGHT_ROWS, KNOTS), F32),
        ],
        compiler_params=params(32),
        name="right_sums",
    )(*parts, design, resid, watt, comps, phase, knots, source_row, codes, sums)


def solve_kernel(prior, got_ref, out_ref, work_ref):
    total = got_ref[0]
    for other in range(1, N_SRC):
        total = total + got_ref[other]
    lane8 = iota((8, OBS), 1)
    sublane8 = iota((8, OBS), 0)
    index = {}
    for i, (p, q) in enumerate(PAIRS):
        index[p, q] = index[q, p] = i
    bands = []
    for spacing in range(4):
        rows = [total[spacing * 10 + i : spacing * 10 + i + 1] for i in range(10)]
        if spacing == 0:
            rows = [row + prior if PAIRS[i][0] == PAIRS[i][1] else row for i, row in enumerate(rows)]
        full = [rows[index[p, q]] for p in range(4) for q in range(4)]
        bands.append([jnp.concatenate(full[:8], axis=0), jnp.concatenate(full[8:], axis=0)])
    right = total[BAND_ROWS : BAND_ROWS + 4]
    right = jnp.concatenate([right, right], axis=0)

    place = jnp.bitwise_and(lane8, 31)
    window_at = jnp.bitwise_and(lane8, 64)
    is_down = jnp.bitwise_and(lane8, 32) != 0

    def arranged(values, spacing, base):
        step = place + base
        up_index = jnp.minimum(window_at + step, OBS - 1)
        down_index = jnp.maximum(window_at + KNOTS - 1 - step, 0)
        up = jnp.take_along_axis(roll(values, spacing, 1), up_index, axis=1)
        down = jnp.take_along_axis(values, down_index, axis=1)
        down = jnp.where(step - spacing >= HALF, 0.0, down)
        return jnp.where(is_down, down, up)

    def entering(base):
        return [arranged(bands[d][h], d, base) for d in range(4) for h in range(2)] + [
            arranged(right, 0, base)
        ]

    stream, tail = entering(0), entering(32)

    lower = sublane8 < 4

    def insert(front, target, pieces, slot, present):
        def part(d, p, half):
            values = pieces[2 * d + p // 2]
            return values if p % 2 == half else roll(values, 4, 0)

        for d in range(1, present + 1):
            other = (slot - d) % 4
            for q in range(4):
                old = front[other * 4 + q]
                fresh = part(d, q, slot % 2)
                keep = lower if slot % 2 == 1 else jnp.logical_not(lower)
                old[slot // 2] = jnp.where(keep, old[slot // 2], fresh)
        for p in range(4):
            halves = []
            for h in range(2):
                both = []
                for spot in range(2):
                    d = (slot - (2 * h + spot)) % 4
                    both.append(part(d, p, spot) if d <= present else jnp.zeros((8, OBS), F32))
                halves.append(jnp.where(lower, both[0], both[1]))
            front[slot * 4 + p] = halves
        keep = lower if slot % 2 == 1 else jnp.logical_not(lower)
        target[slot // 2] = jnp.where(keep, target[slot // 2], pieces[8])

    def eliminate(front, target, slot, gone):
        scale = None
        for p in range(4):
            row = slot * 4 + p
            half, at = row // 8, row % 8
            column = front[row]
            inverse = 1.0 / column[half][at : at + 1, :]
            scale = inverse if scale is None else jnp.where(sublane8 == at, inverse, scale)
            factor = [column[h] * inverse for h in range(2)]
            factor[half] = jnp.where(sublane8 == at, 0.0, factor[half])
            gone = gone | {row}
            for c in [c for c in range(16) if c not in gone] + [16]:
                values = target if c == 16 else front[c]
                pivot = values[half][at : at + 1, :]
                for h in range(2):
                    values[h] = values[h] - factor[h] * pivot
        return gone, scale

    def save(front, target, slot, step, scale):
        for r in range(1, 4):
            for q in range(4):
                work_ref[step * 13 + (r - 1) * 4 + q] = (
                    front[(slot + r) % 4 * 4 + q][slot // 2] * scale
                )
        work_ref[step * 13 + 12] = target[slot // 2] * scale

    zero = jnp.zeros((8, OBS), F32)
    front = [[zero, zero] for _ in range(16)]
    target = [zero, zero]
    for step in range(4):
        insert(front, target, [roll(values, -step, 1) for values in stream], step, step)
    for step in range(HALF):
        slot = step % 4
        unused, scale = eliminate(front, target, slot, frozenset())
        save(front, target, slot, step, scale)
        source, shift = (stream, step + 4) if step < 28 else (tail, step - 28)
        insert(front, target, [roll(values, -shift, 1) for values in source], slot, 3)

    mirror = jnp.bitwise_xor(lane8, 32)

    def mirrored(values):
        return jnp.take_along_axis(roll(values, 4, 0), mirror, axis=1)

    front = [
        [front[a * 4 + p][h] + mirrored(front[(3 - a) * 4 + p][1 - h]) for h in range(2)]
        for a in range(4)
        for p in range(4)
    ]
    target = [target[h] + mirrored(target[1 - h]) for h in range(2)]
    gone = frozenset()
    scales = {}
    for slot in (2, 3, 0, 1):
        gone, scales[slot] = eliminate(front, target, slot, gone)
    target = [
        target[h] * jnp.where(lower, scales[2 * h], scales[2 * h + 1]) for h in range(2)
    ]

    first_lane = place == 0
    placed = []

    def emit(answer, slot, step):
        values = answer[slot // 2]
        values = values if slot % 2 == 0 else roll(values, 4, 0)
        placed.append(roll(jnp.where(first_lane, values, 0.0), step, 1))

    def back(answer, slot, step):
        half = slot // 2
        parts = [work_ref[step * 13 + 12]]
        for r in (3, 2, 1):
            other = (slot + r) % 4
            terms = []
            for q in range(4):
                at = other % 2 * 4 + q
                terms.append(
                    work_ref[step * 13 + (r - 1) * 4 + q] * answer[other // 2][at : at + 1, :]
                )
            parts.append((terms[0] + terms[1]) + (terms[2] + terms[3]))
        fresh = ((parts[0] - parts[1]) - parts[2]) - parts[3]
        keep = lower if slot % 2 == 1 else jnp.logical_not(lower)
        answer[half] = jnp.where(keep, answer[half], fresh)

    answer = list(target)
    emit(answer, 3, 31)
    emit(answer, 2, 30)
    for step in range(HALF - 1, -1, -1):
        back(answer, step % 4, step)
        emit(answer, step % 4, step)
    while len(placed) > 1:
        placed = [placed[i] + placed[i + 1] for i in range(0, len(placed), 2)]
    result = placed[0]
    knot = jnp.bitwise_and(lane8, KNOTS - 1)
    from_lane = jnp.where(knot < 32, lane8, window_at + 32 + KNOTS - 1 - knot)
    panel = jnp.take_along_axis(result, from_lane, axis=1)
    for owner in range(N_SRC):
        out_ref[owner] = panel


def solve_panels(got, prior):
    def body(*refs):
        solve_kernel(prior, *refs)

    return pl.pallas_call(
        body,
        out_shape=jax.ShapeDtypeStruct((N_SRC, 8, OBS), F32),
        in_specs=[VMEM],
        out_specs=VMEM,
        scratch_shapes=[pltpu.VMEM((HALF * 13, 8, OBS), F32)],
        compiler_params=params(16),
        name="solve_panels",
    )(got)


def window_hot_kernel(window_ref, hot_ref):
    window = window_ref[...]
    place = jnp.bitwise_and(window, 1) * N_SRC + lax.shift_right_logical(window, 4)
    row = iota((OBS, BLK_DEV), 0)
    hot = (jnp.bitwise_and(row, N_COL - 1) == place) & (row < 3 * N_COL)
    hot_ref[...] = hot.astype(F32).T


def window_hot(window_row):
    return pl.pallas_call(
        window_hot_kernel,
        out_shape=pltpu.VMEM((BLK_DEV, OBS), F32),
        in_specs=[VMEM],
        out_specs=VMEM,
        compiler_params=params(16),
        name="window_hot",
    )(window_row)


def final_kernel(panel_ref, hot_ref, comp_ref, phase_ref, knot_ref, first_ref, out_ref, table_ref):
    sides = []
    for p in range(4):
        even = panel_ref[pl.ds(p, N_SRC, stride=8), :]
        sides.append(jnp.concatenate([even, roll(even, KNOTS, 1)], axis=0))
    pieces = list(split3(jnp.concatenate(sides, axis=1)))
    pieces = jnp.concatenate(pieces + [jnp.zeros((N_COL, 4 * OBS), BF16)], axis=0)
    for start in range(0, BLK_DEV, OBS):
        table_ref[start : start + OBS, :] = jnp.dot(
            hot_ref[start : start + OBS, :].astype(BF16), pieces, preferred_element_type=F32
        )

    def one_group(group, carry):
        at = pl.ds(pl.multiple_of(group * 8, 8), 8)
        knots = knot_ref[at, :]
        spline = spline_weights(phase_ref[at, :])
        correction = [jnp.zeros((8, OBS), F32) for _ in range(4)]
        for p in range(4):
            table = table_ref[at, p * OBS : (p + 1) * OBS]
            comps = comp_ref[pl.ds(group * 32 + p, 8, stride=4), :]
            for m in range(4):
                picked = jnp.take_along_axis(table, knots + m, axis=1, mode="promise_in_bounds")
                correction[m] = correction[m] + comps * picked
        total = spline[0] * correction[0]
        for m in range(1, 4):
            total = total + spline[m] * correction[m]
        out_ref[at, :] = first_ref[at, :] - total
        return carry

    lax.fori_loop(0, BLK_DEV // 8, one_group, 0, unroll=64)


def final_residual(panels, hot, comps, phase, knots, first):
    return pl.pallas_call(
        final_kernel,
        out_shape=jax.ShapeDtypeStruct((BLK_DEV, OBS), F32),
        in_specs=[VMEM] * 6,
        out_specs=VMEM,
        scratch_shapes=[pltpu.VMEM((BLK_DEV, 4 * OBS), F32)],
        compiler_params=params(16),
        name="final_residual",
    )(panels.reshape(N_SRC * 8, OBS), hot, comps, phase, knots, first)


def shards(
    src_design,
    att_comp,
    spline_phase,
    knot_offset,
    obs_weight,
    residual,
    block_source,
    block_window,
    send_list,
    send_count,
):
    n_win = lax.axis_size("win")
    design = src_design.transpose(1, 0, 2)
    comps = att_comp.reshape(BLK_DEV * 4, OBS)
    source_row = block_source.reshape(1, BLK_DEV)
    obs_src = OBS * BLK_DEV * n_win // SRC_DEV
    obs_win = OBS * BLK_DEV // WIN_SUB
    prior = 0.005 * obs_win / obs_src

    def swap(values, bit):
        return lax.ppermute(values, "win", [(i, i ^ bit) for i in range(n_win)])

    stats = source_sums(design, obs_weight, residual, source_row)
    stats = stats + swap(stats, 1)
    parts = (stats, swap(stats, 2), swap(stats, 4), swap(stats, 6))
    sums, watt, codes = normal_sums(
        comps, spline_phase, knot_offset, obs_weight, send_list, send_count, block_window
    )
    source_step, first, sums = right_sums(
        parts,
        design,
        residual,
        watt,
        comps,
        spline_phase,
        knot_offset,
        source_row,
        codes,
        sums,
    )
    got = lax.all_to_all(sums, "src", split_axis=0, concat_axis=0, tiled=True)
    own_panels = solve_panels(got, prior)
    panels = lax.all_to_all(own_panels, "src", split_axis=0, concat_axis=0, tiled=True)
    attitude_step = (
        own_panels[0, :4].reshape(4, WIN_SUB, KNOTS).transpose(1, 2, 0).reshape(WIN_SUB, KNOTS * 4)
    )
    hot = window_hot(block_window.reshape(1, BLK_DEV))
    last = final_residual(panels, hot, comps, spline_phase, knot_offset, first)
    return (source_step, attitude_step, last)


def solution(mesh):
    return jax.shard_map(
        shards,
        mesh=mesh,
        in_specs=(
            P(("src", "win"), None, None),
            P(("src", "win"), None, None),
            P(("src", "win"), None),
            P(("src", "win"), None),
            P(("src", "win"), None),
            P(("src", "win"), None),
            P(("src", "win")),
            P(("src", "win")),
            P(("src", "win"), None),
            P(("src", "win")),
        ),
        out_specs=(P(None, "src"), P(("src", "win"), None), P(("src", "win"), None)),
        check_vma=False,
    )
```

```python
import jax
import jax.numpy as jnp
from jax import lax
from jax.experimental import pallas as pl
from jax.experimental.pallas import tpu as pltpu
from jax.sharding import PartitionSpec as P

OBS = 128
KNOTS = 64
WIN_SUB = 2
BLK_DEV = 512
SRC_DEV = 256
N_SRC = 16
N_COL = N_SRC * WIN_SUB
HALF = 30
PAIRS = [(p, q) for p in range(4) for q in range(p, 4)]
PAIR_ROWS = 8 * len(PAIRS)
RIGHT_ROWS = 16
BAND_ROWS = 4 * len(PAIRS)
ROWS = 48
STAT_ROWS = 24
CODES = 384
N_PAIR = 272
NO_BLOCK = 512
F32 = jnp.float32
BF16 = jnp.bfloat16
NT = (((1,), (1,)), ((), ()))
SPLINE = [
    [1 / 6, 0.0, 0.0, 0.0],
    [4 / 6, 12 / 6, 6 / 6, 1 / 6],
    [1 / 6, 6 / 6, 12 / 6, 4 / 6],
    [0.0, 0.0, 0.0, 1 / 6],
]


def iota(shape, dim):
    return lax.broadcasted_iota(jnp.int32, shape, dim)


def split2(values):
    high = values.astype(BF16)
    return high, (values - high.astype(F32)).astype(BF16)


def split3(values):
    high = values.astype(BF16)
    rest = values - high.astype(F32)
    mid = rest.astype(BF16)
    return high, mid, (rest - mid.astype(F32)).astype(BF16)


def spline_weights(phase):
    square = phase * phase
    cube = square * phase
    rest = 1.0 - phase
    return [
        rest * rest * rest * (1.0 / 6.0),
        (3.0 * cube - 6.0 * square + 4.0) * (1.0 / 6.0),
        (-3.0 * cube + 3.0 * square + 3.0 * phase + 1.0) * (1.0 / 6.0),
        cube * (1.0 / 6.0),
    ]


def params(megabytes):
    return pltpu.CompilerParams(vmem_limit_bytes=int(megabytes * 1024 * 1024))


VMEM = pl.BlockSpec(memory_space=pltpu.VMEM)
SMEM = pl.BlockSpec(memory_space=pltpu.SMEM)
HBM = pl.BlockSpec(memory_space=pltpu.HBM)


def column_window(window_ref, block):
    window = window_ref[block]
    return lax.shift_right_logical(window, 4) * 2 + jnp.bitwise_and(window, 1)


def stats_kernel(
    design_in, weight_in, resid_in, source_ref, out_ref, design_ref, weight_ref, resid_ref, sums_ref, sems
):
    chunks = 4
    size = BLK_DEV // chunks
    copies = []
    for chunk in range(chunks):
        at = pl.ds(chunk * size, size)
        copies.append(
            [
                pltpu.make_async_copy(design_in.at[:, at], design_ref.at[:, at], sems.at[chunk, 0]),
                pltpu.make_async_copy(weight_in.at[at], weight_ref.at[at], sems.at[chunk, 1]),
                pltpu.make_async_copy(resid_in.at[at], resid_ref.at[at], sems.at[chunk, 2]),
            ]
        )
        for copy in copies[chunk]:
            copy.start()
    rows = 32
    lane = iota((rows, OBS), 1)
    for chunk in range(chunks):
        for copy in copies[chunk]:
            copy.wait()
        for group in range(size // rows):
            at = pl.ds(chunk * size + group * rows, rows)
            weight = weight_ref[at, :]
            design = [design_ref[p, at, :] for p in range(5)]
            resid = resid_ref[at, :]
            weighted = [weight * design[p] for p in range(5)]
            packed = jnp.zeros((rows, OBS), F32)
            slot = 0
            for p in range(5):
                for q in range(p + 1):
                    total = jnp.sum(weighted[p] * design[q], axis=1, keepdims=True)
                    packed = jnp.where(lane == slot, total, packed)
                    slot += 1
            for p in range(5):
                total = jnp.sum(weighted[p] * resid, axis=1, keepdims=True)
                packed = jnp.where(lane == slot, total, packed)
                slot += 1
            sums_ref[at, :] = packed
    local = jnp.bitwise_and(source_ref[...], SRC_DEV - 1)
    hot = (iota((SRC_DEV, BLK_DEV), 0) == local).astype(F32).astype(BF16)
    total = jnp.zeros((SRC_DEV, OBS), F32)
    for piece in split3(sums_ref[...]):
        total = total + jnp.dot(hot, piece, preferred_element_type=F32)
    out_ref[...] = total.T[:STAT_ROWS]


def source_sums(design, weight, resid, source_row):
    return pl.pallas_call(
        stats_kernel,
        out_shape=pltpu.VMEM((STAT_ROWS, SRC_DEV), F32),
        in_specs=[HBM] * 3 + [VMEM],
        out_specs=VMEM,
        scratch_shapes=[
            pltpu.VMEM((5, BLK_DEV, OBS), F32),
            pltpu.VMEM((BLK_DEV, OBS), F32),
            pltpu.VMEM((BLK_DEV, OBS), F32),
            pltpu.VMEM((BLK_DEV, OBS), F32),
            pltpu.SemaphoreType.DMA((4, 3)),
        ],
        compiler_params=params(54),
        name="source_sums",
    )(*(pltpu.with_memory_space_constraint(x, pltpu.HBM) for x in (design, weight, resid)), source_row)


def roll(values, amount, axis):
    size = values.shape[axis]
    return pltpu.roll(values, amount % size, axis) if amount % size else values


def convolved(first, second):
    out = [0.0] * 7
    for i in range(4):
        for j in range(4):
            out[i + j] += SPLINE[first][i] * SPLINE[second][j]
    return out


def fold_bands(term_ref, out_ref):
    low_terms = [term_ref[pl.ds(k, 8, stride=8), :] for k in range(7)]
    high_terms = [term_ref[pl.ds(64 + k, 2, stride=8), :] for k in range(7)]
    for spacing in range(4):
        low = high = None
        for first in range(4 - spacing):
            low_slot = high_slot = None
            for k, weight in enumerate(convolved(first, first + spacing)):
                if weight != 0.0:
                    low_slot = plus(low_slot, weight * low_terms[k])
                    high_slot = plus(high_slot, weight * high_terms[k])
            low = plus(low, roll(low_slot, first, 1))
            high = plus(high, roll(high_slot, first, 1))
        out_ref[spacing * 10 : spacing * 10 + 8, :] = low
        out_ref[spacing * 10 + 8 : spacing * 10 + 10, :] = high


def plus(total, value):
    return value if total is None else total + value


def pair_members(code_ref, pair):
    code = code_ref[0, pair]
    blocks = []
    for shift in (0, 10):
        block = jnp.bitwise_and(lax.shift_right_logical(code, shift), 1023)
        blocks.append((jnp.minimum(block, BLK_DEV - 1), jnp.bitwise_and(block, NO_BLOCK)))
    return lax.shift_right_logical(code, 20), blocks


def pair_codes(window):
    column = lax.shift_right_logical(window, 4) * 2 + jnp.bitwise_and(window, 1)
    hot = (iota((N_COL, BLK_DEV), 0) == column).astype(F32)
    before = (iota((OBS, OBS), 0) < iota((OBS, OBS), 1)).astype(F32).astype(BF16)
    count = jnp.zeros((N_COL, 1), F32)
    ranks = []
    for start in range(0, BLK_DEV, OBS):
        part = hot[:, start : start + OBS]
        seen = jnp.dot(part.astype(BF16), before, preferred_element_type=F32) + count
        ranks.append(jnp.sum(part * seen, axis=0, keepdims=True))
        count = count + jnp.sum(part, axis=1, keepdims=True)
    rank = jnp.concatenate(ranks, axis=1).astype(jnp.int32)
    pairs = lax.shift_right_logical(count.astype(jnp.int32) + 1, 1).astype(F32)
    below = (iota((N_COL, N_COL), 1) < iota((N_COL, N_COL), 0)).astype(F32).astype(BF16)
    spread = jnp.broadcast_to(pairs, (N_COL, OBS)).astype(BF16)
    start = jnp.dot(below, spread, preferred_element_type=F32)[:, :1]
    pair = jnp.sum(hot * start, axis=0, keepdims=True).astype(jnp.int32)
    pair = pair + lax.shift_right_logical(rank, 1)
    second = jnp.bitwise_and(rank, 1)
    missing = NO_BLOCK - iota((1, BLK_DEV), 1)
    high, low = lax.shift_right_logical(missing, 4), jnp.bitwise_and(missing, 15)
    first = 1 - second
    rows = [first * high, first * low, second * high, second * low, first * column]
    rows = jnp.concatenate([row.astype(F32) for row in rows] + [jnp.zeros((11, BLK_DEV), F32)], axis=0)
    target = (iota((CODES, BLK_DEV), 0) == pair).astype(F32).astype(BF16)
    found = lax.dot_general(rows.astype(BF16), target, NT, preferred_element_type=F32)
    found = found.astype(jnp.int32)
    left = NO_BLOCK - found[0:1] * 16 - found[1:2]
    right = NO_BLOCK - found[2:3] * 16 - found[3:4]
    return left + right * 1024 + found[4:5] * (1 << 20)


def knots_hot(knot_ref, block, offset):
    hot = iota((KNOTS, OBS), 0) == knot_ref[pl.ds(block, 1), :] + offset
    return hot.astype(F32).astype(BF16)


def normals_kernel(
    comp_ref,
    phase_ref,
    knot_ref,
    weight_ref,
    list_ref,
    window_row_ref,
    count_ref,
    window_ref,
    out_ref,
    watt_ref,
    code_ref,
    poly_ref,
    pair_ref,
    total_ref,
    joined_ref,
):
    code_ref[...] = pair_codes(window_row_ref[...])
    named = jnp.zeros((16, BLK_DEV // 8), F32)
    capacity = list_ref.shape[1]
    slot = iota((1, capacity), 1)
    for owner in range(N_SRC):
        entry = jnp.where(slot < count_ref[owner], list_ref[owner : owner + 1, :], -1)
        group_hot = iota((BLK_DEV // 8, capacity), 0) == lax.shift_right_arithmetic(entry, 3)
        place_hot = iota((16, capacity), 0) == jnp.where(entry < 0, -1, jnp.bitwise_and(entry, 7))
        named = named + lax.dot_general(
            place_hot.astype(F32).astype(BF16),
            group_hot.astype(F32).astype(BF16),
            NT,
            preferred_element_type=F32,
        )
    named = jnp.concatenate([named[:8], jnp.zeros((8, OBS - BLK_DEV // 8), F32)], axis=1)

    def prepare(group, carry):
        at = pl.ds(pl.multiple_of(group * 8, 8), 8)
        phase = phase_ref[at, :]
        rest = 1.0 - phase
        up = [None, phase, phase * phase, None]
        down = [None, rest, rest * rest, None]
        up[3] = up[2] * phase
        down[3] = down[2] * rest
        poly = [
            down[3] * down[3],
            phase * (down[3] * down[2]),
            up[2] * (down[2] * down[2]),
            up[3] * down[3],
            (up[2] * up[2]) * down[2],
            (up[3] * up[2]) * rest,
            up[3] * up[3],
            jnp.zeros_like(phase),
        ]
        for k in range(8):
            poly_ref[pl.ds(group * 64 + k, 8, stride=8), :] = poly[k]
        times = jnp.take_along_axis(named, jnp.full((8, OBS), group, jnp.int32), axis=1)
        weight = weight_ref[at, :] * times
        watt_ref[at, :] = weight
        comps = [comp_ref[pl.ds(group * 32 + p, 8, stride=4), :] for p in range(4)]
        weighted = [weight * comps[p] for p in range(4)]
        for i, (p, q) in enumerate(PAIRS):
            pair_ref[i, at, :] = weighted[p] * comps[q]
        return carry

    lax.fori_loop(0, BLK_DEV // 8, prepare, 0, unroll=64)
    total_ref[...] = jnp.zeros_like(total_ref)
    unrolled = 256

    def one_group(group, carry):
        for i in range(unrolled):
            block = group * unrolled + i
            poly = poly_ref[pl.ds(pl.multiple_of(block * 8, 8), 8), :]
            terms = jnp.concatenate(
                [poly * pair_ref[n, pl.ds(block, 1), :] for n in range(len(PAIRS))], axis=0
            )
            hot = knots_hot(knot_ref, block, 0)
            summed = lax.dot_general(
                jnp.concatenate(split2(terms), axis=1),
                jnp.concatenate([hot, hot], axis=1),
                NT,
                preferred_element_type=F32,
            )
            column = column_window(window_ref, block)
            total_ref[column] = total_ref[column] + summed
        return carry

    lax.fori_loop(0, BLK_DEV // unrolled, one_group, 0)
    for owner in range(N_SRC):
        joined_ref[owner, :, :] = jnp.concatenate(
            [total_ref[2 * owner], total_ref[2 * owner + 1]], axis=1
        )
    for owner in range(N_SRC):
        fold_bands(joined_ref.at[owner], out_ref.at[owner])


def normal_sums(comps, phase, knots, weight, lists, counts, window):
    return pl.pallas_call(
        normals_kernel,
        out_shape=(
            jax.ShapeDtypeStruct((N_SRC, BAND_ROWS, OBS), F32),
            jax.ShapeDtypeStruct((BLK_DEV, OBS), F32),
            jax.ShapeDtypeStruct((1, CODES), jnp.int32),
        ),
        in_specs=[VMEM] * 6 + [SMEM] * 2,
        out_specs=(VMEM, VMEM, VMEM),
        scratch_shapes=[
            pltpu.VMEM((BLK_DEV * 8, OBS), F32),
            pltpu.VMEM((len(PAIRS), BLK_DEV, OBS), F32),
            pltpu.VMEM((N_COL, PAIR_ROWS, KNOTS), F32),
            pltpu.VMEM((N_SRC, PAIR_ROWS, OBS), F32),
        ],
        compiler_params=params(32),
        cost_estimate=pl.CostEstimate(flops=3_000_000_000, bytes_accessed=4_000_000, transcendentals=0),
        name="normal_sums",
    )(comps, phase, knots, weight, lists, window.reshape(1, BLK_DEV), counts, window)


def solve_five(totals):
    def entry_at(across, within):
        row = across * (across + 1) // 2 + within
        return totals[row : row + 1, :]

    factor = {}
    inverse = {}
    for across in range(5):
        for within in range(across + 1):
            entry = entry_at(across, within)
            if across == within:
                entry = entry + 1.0
            for before in range(within):
                entry = entry - factor[across, before] * factor[within, before]
            if across == within:
                inverse[across] = 1.0 / jnp.sqrt(entry)
            else:
                factor[across, within] = entry * inverse[within]
    forward = []
    for across in range(5):
        entry = totals[15 + across : 16 + across, :]
        for before in range(across):
            entry = entry - factor[across, before] * forward[before]
        forward.append(entry * inverse[across])
    backward = [None] * 5
    for across in range(4, -1, -1):
        entry = forward[across]
        for later in range(across + 1, 5):
            entry = entry - factor[later, across] * backward[later]
        backward[across] = entry * inverse[across]
    return backward


def rights_kernel(
    own_ref,
    near_ref,
    far_ref,
    cross_ref,
    design_ref,
    resid_ref,
    watt_ref,
    comp_ref,
    phase_ref,
    knot_ref,
    source_ref,
    code_ref,
    bands_ref,
    step_ref,
    first_ref,
    sums_ref,
    column_ref,
    term_ref,
    total_ref,
):
    totals = (own_ref[...] + near_ref[...]) + (far_ref[...] + cross_ref[...])
    step = solve_five(totals)
    for p in range(5):
        step_ref[p : p + 1, :] = step[p]
    stacked = jnp.concatenate(step + [jnp.zeros((3, SRC_DEV), F32)], axis=0)
    pieces = jnp.concatenate(list(split3(stacked)) + [jnp.zeros((8, SRC_DEV), BF16)], axis=0)
    local = jnp.bitwise_and(source_ref[...], SRC_DEV - 1)
    hot = (iota((SRC_DEV, BLK_DEV), 0) == local).astype(F32).astype(BF16)
    picked = jnp.dot(pieces, hot, preferred_element_type=F32)
    picked = picked[:8] + picked[8:16] + picked[16:24]
    column_ref[...] = jnp.concatenate([picked, jnp.zeros((OBS - 8, BLK_DEV), F32)], axis=0).T

    def prepare(group, carry):
        at = pl.ds(pl.multiple_of(group * 8, 8), 8)
        columns = column_ref[at, :]
        fitted = jnp.zeros((8, OBS), F32)
        for p in range(5):
            fitted = fitted + design_ref[p, at, :] * columns[:, p : p + 1]
        first = resid_ref[at, :] - fitted
        first_ref[at, :] = first
        weighted = watt_ref[at, :] * first
        spline = spline_weights(phase_ref[at, :])
        comps = [comp_ref[pl.ds(group * 32 + p, 8, stride=4), :] for p in range(4)]
        for m in range(4):
            scaled = weighted * spline[m]
            for p in range(4):
                term_ref[pl.ds(group * 128 + 4 * m + p, 8, stride=16), :] = scaled * comps[p]
        return carry

    lax.fori_loop(0, BLK_DEV // 8, prepare, 0, unroll=64)
    total_ref[...] = jnp.zeros_like(total_ref)
    unrolled = 272

    def one_group(group, carry):
        for i in range(unrolled):
            at, blocks = pair_members(code_ref, group * unrolled + i)
            sides = []
            for block, offset in blocks:
                terms = term_ref[pl.ds(pl.multiple_of(block * 16, 16), 16), :]
                sides.append(
                    (jnp.concatenate(split2(terms), axis=0), knots_hot(knot_ref, block, offset))
                )
            summed = lax.dot_general(
                jnp.concatenate([sides[0][0], sides[1][0]], axis=1),
                jnp.concatenate([sides[0][1], sides[1][1]], axis=1),
                NT,
                preferred_element_type=F32,
            )
            total_ref[at] = total_ref[at] + (summed[:RIGHT_ROWS] + summed[RIGHT_ROWS:])
        return carry

    lax.fori_loop(0, N_PAIR // unrolled, one_group, 0)
    for owner in range(N_SRC):
        joined = jnp.concatenate([total_ref[2 * owner], total_ref[2 * owner + 1]], axis=1)
        right = joined[:4]
        for first in range(1, 4):
            right = right + roll(joined[4 * first : 4 * first + 4], first, 1)
        sums_ref[owner, :BAND_ROWS, :] = bands_ref[owner]
        sums_ref[owner, BAND_ROWS:, :] = jnp.concatenate([right, jnp.zeros((4, OBS), F32)], axis=0)


def right_sums(parts, design, resid, watt, comps, phase, knots, source_row, codes, sums):
    return pl.pallas_call(
        rights_kernel,
        out_shape=(
            jax.ShapeDtypeStruct((5, SRC_DEV), F32),
            jax.ShapeDtypeStruct((BLK_DEV, OBS), F32),
            jax.ShapeDtypeStruct((N_SRC, ROWS, OBS), F32),
        ),
        in_specs=[VMEM] * 11 + [SMEM, VMEM],
        out_specs=(VMEM, VMEM, VMEM),
        scratch_shapes=[
            pltpu.VMEM((BLK_DEV, OBS), F32),
            pltpu.VMEM((BLK_DEV * 16, OBS), F32),
            pltpu.VMEM((N_COL, RIGHT_ROWS, KNOTS), F32),
        ],
        compiler_params=params(32),
        name="right_sums",
    )(*parts, design, resid, watt, comps, phase, knots, source_row, codes, sums)


def solve_kernel(prior, got_ref, out_ref, work_ref):
    total = got_ref[0]
    for other in range(1, N_SRC):
        total = total + got_ref[other]
    lane8 = iota((8, OBS), 1)
    sublane8 = iota((8, OBS), 0)
    index = {}
    for i, (p, q) in enumerate(PAIRS):
        index[p, q] = index[q, p] = i
    bands = []
    for spacing in range(4):
        rows = [total[spacing * 10 + i : spacing * 10 + i + 1] for i in range(10)]
        if spacing == 0:
            rows = [row + prior if PAIRS[i][0] == PAIRS[i][1] else row for i, row in enumerate(rows)]
        full = [rows[index[p, q]] for p in range(4) for q in range(4)]
        bands.append([jnp.concatenate(full[:8], axis=0), jnp.concatenate(full[8:], axis=0)])
    right = total[BAND_ROWS : BAND_ROWS + 4]
    right = jnp.concatenate([right, right], axis=0)

    place = jnp.bitwise_and(lane8, 31)
    window_at = jnp.bitwise_and(lane8, 64)
    is_down = jnp.bitwise_and(lane8, 32) != 0

    def arranged(values, spacing, base):
        step = place + base
        up_index = jnp.minimum(window_at + step, OBS - 1)
        down_index = jnp.maximum(window_at + KNOTS - 1 - step, 0)
        up = jnp.take_along_axis(roll(values, spacing, 1), up_index, axis=1)
        down = jnp.take_along_axis(values, down_index, axis=1)
        down = jnp.where(step - spacing >= HALF, 0.0, down)
        return jnp.where(is_down, down, up)

    def entering(base):
        return [arranged(bands[d][h], d, base) for d in range(4) for h in range(2)] + [
            arranged(right, 0, base)
        ]

    stream, tail = entering(0), entering(32)

    lower = sublane8 < 4

    def insert(front, target, pieces, slot, present):
        def part(d, p, half):
            values = pieces[2 * d + p // 2]
            return values if p % 2 == half else roll(values, 4, 0)

        for d in range(1, present + 1):
            other = (slot - d) % 4
            for q in range(4):
                old = front[other * 4 + q]
                fresh = part(d, q, slot % 2)
                keep = lower if slot % 2 == 1 else jnp.logical_not(lower)
                old[slot // 2] = jnp.where(keep, old[slot // 2], fresh)
        for p in range(4):
            halves = []
            for h in range(2):
                both = []
                for spot in range(2):
                    d = (slot - (2 * h + spot)) % 4
                    both.append(part(d, p, spot) if d <= present else jnp.zeros((8, OBS), F32))
                halves.append(jnp.where(lower, both[0], both[1]))
            front[slot * 4 + p] = halves
        keep = lower if slot % 2 == 1 else jnp.logical_not(lower)
        target[slot // 2] = jnp.where(keep, target[slot // 2], pieces[8])

    def eliminate(front, target, slot, gone):
        scale = None
        for p in range(4):
            row = slot * 4 + p
            half, at = row // 8, row % 8
            column = front[row]
            inverse = 1.0 / column[half][at : at + 1, :]
            scale = inverse if scale is None else jnp.where(sublane8 == at, inverse, scale)
            factor = [column[h] * inverse for h in range(2)]
            factor[half] = jnp.where(sublane8 == at, 0.0, factor[half])
            gone = gone | {row}
            for c in [c for c in range(16) if c not in gone] + [16]:
                values = target if c == 16 else front[c]
                pivot = values[half][at : at + 1, :]
                for h in range(2):
                    values[h] = values[h] - factor[h] * pivot
        return gone, scale

    def save(front, target, slot, step, scale):
        for r in range(1, 4):
            for q in range(4):
                work_ref[step * 13 + (r - 1) * 4 + q] = (
                    front[(slot + r) % 4 * 4 + q][slot // 2] * scale
                )
        work_ref[step * 13 + 12] = target[slot // 2] * scale

    zero = jnp.zeros((8, OBS), F32)
    front = [[zero, zero] for _ in range(16)]
    target = [zero, zero]
    for step in range(4):
        insert(front, target, [roll(values, -step, 1) for values in stream], step, step)
    for step in range(HALF):
        slot = step % 4
        unused, scale = eliminate(front, target, slot, frozenset())
        save(front, target, slot, step, scale)
        source, shift = (stream, step + 4) if step < 28 else (tail, step - 28)
        insert(front, target, [roll(values, -shift, 1) for values in source], slot, 3)

    mirror = jnp.bitwise_xor(lane8, 32)

    def mirrored(values):
        return jnp.take_along_axis(roll(values, 4, 0), mirror, axis=1)

    front = [
        [front[a * 4 + p][h] + mirrored(front[(3 - a) * 4 + p][1 - h]) for h in range(2)]
        for a in range(4)
        for p in range(4)
    ]
    target = [target[h] + mirrored(target[1 - h]) for h in range(2)]
    gone = frozenset()
    scales = {}
    for slot in (2, 3, 0, 1):
        gone, scales[slot] = eliminate(front, target, slot, gone)
    target = [
        target[h] * jnp.where(lower, scales[2 * h], scales[2 * h + 1]) for h in range(2)
    ]

    first_lane = place == 0
    placed = []

    def emit(answer, slot, step):
        values = answer[slot // 2]
        values = values if slot % 2 == 0 else roll(values, 4, 0)
        placed.append(roll(jnp.where(first_lane, values, 0.0), step, 1))

    def back(answer, slot, step):
        half = slot // 2
        parts = [work_ref[step * 13 + 12]]
        for r in (3, 2, 1):
            other = (slot + r) % 4
            terms = []
            for q in range(4):
                at = other % 2 * 4 + q
                terms.append(
                    work_ref[step * 13 + (r - 1) * 4 + q] * answer[other // 2][at : at + 1, :]
                )
            parts.append((terms[0] + terms[1]) + (terms[2] + terms[3]))
        fresh = ((parts[0] - parts[1]) - parts[2]) - parts[3]
        keep = lower if slot % 2 == 1 else jnp.logical_not(lower)
        answer[half] = jnp.where(keep, answer[half], fresh)

    answer = list(target)
    emit(answer, 3, 31)
    emit(answer, 2, 30)
    for step in range(HALF - 1, -1, -1):
        back(answer, step % 4, step)
        emit(answer, step % 4, step)
    while len(placed) > 1:
        placed = [placed[i] + placed[i + 1] for i in range(0, len(placed), 2)]
    result = placed[0]
    knot = jnp.bitwise_and(lane8, KNOTS - 1)
    from_lane = jnp.where(knot < 32, lane8, window_at + 32 + KNOTS - 1 - knot)
    panel = jnp.take_along_axis(result, from_lane, axis=1)
    for owner in range(N_SRC):
        out_ref[owner] = panel


def solve_panels(got, prior):
    def body(*refs):
        solve_kernel(prior, *refs)

    return pl.pallas_call(
        body,
        out_shape=jax.ShapeDtypeStruct((N_SRC, 8, OBS), F32),
        in_specs=[VMEM],
        out_specs=VMEM,
        scratch_shapes=[pltpu.VMEM((HALF * 13, 8, OBS), F32)],
        compiler_params=params(16),
        name="solve_panels",
    )(got)


def window_hot_kernel(window_ref, hot_ref):
    window = window_ref[...]
    place = jnp.bitwise_and(window, 1) * N_SRC + lax.shift_right_logical(window, 4)
    row = iota((OBS, BLK_DEV), 0)
    hot = (jnp.bitwise_and(row, N_COL - 1) == place) & (row < 3 * N_COL)
    hot_ref[...] = hot.astype(F32).T


def window_hot(window_row):
    return pl.pallas_call(
        window_hot_kernel,
        out_shape=pltpu.VMEM((BLK_DEV, OBS), F32),
        in_specs=[VMEM],
        out_specs=VMEM,
        compiler_params=params(16),
        name="window_hot",
    )(window_row)


def final_kernel(panel_ref, hot_ref, comp_ref, phase_ref, knot_ref, first_ref, out_ref, table_ref):
    sides = []
    for p in range(4):
        even = panel_ref[pl.ds(p, N_SRC, stride=8), :]
        sides.append(jnp.concatenate([even, roll(even, KNOTS, 1)], axis=0))
    pieces = list(split3(jnp.concatenate(sides, axis=1)))
    pieces = jnp.concatenate(pieces + [jnp.zeros((N_COL, 4 * OBS), BF16)], axis=0)
    for start in range(0, BLK_DEV, OBS):
        table_ref[start : start + OBS, :] = jnp.dot(
            hot_ref[start : start + OBS, :].astype(BF16), pieces, preferred_element_type=F32
        )

    def one_group(group, carry):
        at = pl.ds(pl.multiple_of(group * 8, 8), 8)
        knots = knot_ref[at, :]
        spline = spline_weights(phase_ref[at, :])
        correction = [jnp.zeros((8, OBS), F32) for _ in range(4)]
        for p in range(4):
            table = table_ref[at, p * OBS : (p + 1) * OBS]
            comps = comp_ref[pl.ds(group * 32 + p, 8, stride=4), :]
            for m in range(4):
                picked = jnp.take_along_axis(table, knots + m, axis=1, mode="promise_in_bounds")
                correction[m] = correction[m] + comps * picked
        total = spline[0] * correction[0]
        for m in range(1, 4):
            total = total + spline[m] * correction[m]
        out_ref[at, :] = first_ref[at, :] - total
        return carry

    lax.fori_loop(0, BLK_DEV // 8, one_group, 0, unroll=64)


def final_residual(panels, hot, comps, phase, knots, first):
    return pl.pallas_call(
        final_kernel,
        out_shape=jax.ShapeDtypeStruct((BLK_DEV, OBS), F32),
        in_specs=[VMEM] * 6,
        out_specs=VMEM,
        scratch_shapes=[pltpu.VMEM((BLK_DEV, 4 * OBS), F32)],
        compiler_params=params(16),
        name="final_residual",
    )(panels.reshape(N_SRC * 8, OBS), hot, comps, phase, knots, first)


def shards(
    src_design,
    att_comp,
    spline_phase,
    knot_offset,
    obs_weight,
    residual,
    block_source,
    block_window,
    send_list,
    send_count,
):
    n_win = lax.axis_size("win")
    design = src_design.transpose(1, 0, 2)
    comps = att_comp.reshape(BLK_DEV * 4, OBS)
    source_row = block_source.reshape(1, BLK_DEV)
    obs_src = OBS * BLK_DEV * n_win // SRC_DEV
    obs_win = OBS * BLK_DEV // WIN_SUB
    prior = 0.005 * obs_win / obs_src

    def swap(values, bit):
        return lax.ppermute(values, "win", [(i, i ^ bit) for i in range(n_win)])

    stats = source_sums(design, obs_weight, residual, source_row)
    stats = stats + swap(stats, 1)
    parts = (stats, swap(stats, 2), swap(stats, 4), swap(stats, 6))
    sums, watt, codes = normal_sums(
        comps, spline_phase, knot_offset, obs_weight, send_list, send_count, block_window
    )
    source_step, first, sums = right_sums(
        parts,
        design,
        residual,
        watt,
        comps,
        spline_phase,
        knot_offset,
        source_row,
        codes,
        sums,
    )
    got = lax.all_to_all(sums, "src", split_axis=0, concat_axis=0, tiled=True)
    own_panels = solve_panels(got, prior)
    panels = lax.all_to_all(own_panels, "src", split_axis=0, concat_axis=0, tiled=True)
    attitude_step = (
        own_panels[0, :4].reshape(4, WIN_SUB, KNOTS).transpose(1, 2, 0).reshape(WIN_SUB, KNOTS * 4)
    )
    hot = window_hot(block_window.reshape(1, BLK_DEV))
    last = final_residual(panels, hot, comps, spline_phase, knot_offset, first)
    return (source_step, attitude_step, last)


def solution(mesh):
    return jax.shard_map(
        shards,
        mesh=mesh,
        in_specs=(
            P(("src", "win"), None, None),
            P(("src", "win"), None, None),
            P(("src", "win"), None),
            P(("src", "win"), None),
            P(("src", "win"), None),
            P(("src", "win"), None),
            P(("src", "win")),
            P(("src", "win")),
            P(("src", "win"), None),
            P(("src", "win")),
        ),
        out_specs=(P(None, "src"), P(("src", "win"), None), P(("src", "win"), None)),
        check_vma=False,
    )
```

```python
import jax
import jax.numpy as jnp
from jax import lax
from jax.experimental import pallas as pl
from jax.experimental.pallas import tpu as pltpu
from jax.sharding import PartitionSpec as P

OBS = 128
KNOTS = 64
WIN_SUB = 2
BLK_DEV = 512
SRC_DEV = 256
N_SRC = 16
N_COL = N_SRC * WIN_SUB
HALF = 30
PAIRS = [(p, q) for p in range(4) for q in range(p, 4)]
PAIR_ROWS = 8 * len(PAIRS)
RIGHT_ROWS = 16
BAND_ROWS = 4 * len(PAIRS)
ROWS = 48
STAT_ROWS = 24
CODES = 384
N_PAIR = 272
NO_BLOCK = 512
F32 = jnp.float32
BF16 = jnp.bfloat16
NT = (((1,), (1,)), ((), ()))
SPLINE = [
    [1 / 6, 0.0, 0.0, 0.0],
    [4 / 6, 12 / 6, 6 / 6, 1 / 6],
    [1 / 6, 6 / 6, 12 / 6, 4 / 6],
    [0.0, 0.0, 0.0, 1 / 6],
]


def iota(shape, dim):
    return lax.broadcasted_iota(jnp.int32, shape, dim)


def split2(values):
    high = values.astype(BF16)
    return high, (values - high.astype(F32)).astype(BF16)


def split3(values):
    high = values.astype(BF16)
    rest = values - high.astype(F32)
    mid = rest.astype(BF16)
    return high, mid, (rest - mid.astype(F32)).astype(BF16)


def spline_weights(phase):
    square = phase * phase
    cube = square * phase
    rest = 1.0 - phase
    return [
        rest * rest * rest * (1.0 / 6.0),
        (3.0 * cube - 6.0 * square + 4.0) * (1.0 / 6.0),
        (-3.0 * cube + 3.0 * square + 3.0 * phase + 1.0) * (1.0 / 6.0),
        cube * (1.0 / 6.0),
    ]


def params(megabytes):
    return pltpu.CompilerParams(vmem_limit_bytes=int(megabytes * 1024 * 1024))


VMEM = pl.BlockSpec(memory_space=pltpu.VMEM)
SMEM = pl.BlockSpec(memory_space=pltpu.SMEM)
HBM = pl.BlockSpec(memory_space=pltpu.HBM)


def column_window(window_ref, block):
    window = window_ref[block]
    return lax.shift_right_logical(window, 4) * 2 + jnp.bitwise_and(window, 1)


def stats_kernel(
    design_in, weight_in, resid_in, source_ref, out_ref, design_ref, weight_ref, resid_ref, sums_ref, sems
):
    chunks = 4
    size = BLK_DEV // chunks
    copies = []
    for chunk in range(chunks):
        at = pl.ds(chunk * size, size)
        copies.append(
            [
                pltpu.make_async_copy(design_in.at[:, at], design_ref.at[:, at], sems.at[chunk, 0]),
                pltpu.make_async_copy(weight_in.at[at], weight_ref.at[at], sems.at[chunk, 1]),
                pltpu.make_async_copy(resid_in.at[at], resid_ref.at[at], sems.at[chunk, 2]),
            ]
        )
        for copy in copies[chunk]:
            copy.start()
    rows = 32
    lane = iota((rows, OBS), 1)
    for chunk in range(chunks):
        for copy in copies[chunk]:
            copy.wait()
        for group in range(size // rows):
            at = pl.ds(chunk * size + group * rows, rows)
            weight = weight_ref[at, :]
            design = [design_ref[p, at, :] for p in range(5)]
            resid = resid_ref[at, :]
            weighted = [weight * design[p] for p in range(5)]
            packed = jnp.zeros((rows, OBS), F32)
            slot = 0
            for p in range(5):
                for q in range(p + 1):
                    total = jnp.sum(weighted[p] * design[q], axis=1, keepdims=True)
                    packed = jnp.where(lane == slot, total, packed)
                    slot += 1
            for p in range(5):
                total = jnp.sum(weighted[p] * resid, axis=1, keepdims=True)
                packed = jnp.where(lane == slot, total, packed)
                slot += 1
            sums_ref[at, :] = packed
    local = jnp.bitwise_and(source_ref[...], SRC_DEV - 1)
    hot = (iota((SRC_DEV, BLK_DEV), 0) == local).astype(F32).astype(BF16)
    total = jnp.zeros((SRC_DEV, OBS), F32)
    for piece in split3(sums_ref[...]):
        total = total + jnp.dot(hot, piece, preferred_element_type=F32)
    out_ref[...] = total.T[:STAT_ROWS]


def source_sums(design, weight, resid, source_row):
    return pl.pallas_call(
        stats_kernel,
        out_shape=pltpu.VMEM((STAT_ROWS, SRC_DEV), F32),
        in_specs=[HBM] * 3 + [VMEM],
        out_specs=VMEM,
        scratch_shapes=[
            pltpu.VMEM((5, BLK_DEV, OBS), F32),
            pltpu.VMEM((BLK_DEV, OBS), F32),
            pltpu.VMEM((BLK_DEV, OBS), F32),
            pltpu.VMEM((BLK_DEV, OBS), F32),
            pltpu.SemaphoreType.DMA((4, 3)),
        ],
        compiler_params=params(54),
        name="source_sums",
    )(*(pltpu.with_memory_space_constraint(x, pltpu.HBM) for x in (design, weight, resid)), source_row)


def roll(values, amount, axis):
    size = values.shape[axis]
    return pltpu.roll(values, amount % size, axis) if amount % size else values


def convolved(first, second):
    out = [0.0] * 7
    for i in range(4):
        for j in range(4):
            out[i + j] += SPLINE[first][i] * SPLINE[second][j]
    return out


def fold_bands(term_ref, out_ref):
    low_terms = [term_ref[pl.ds(k, 8, stride=8), :] for k in range(7)]
    high_terms = [term_ref[pl.ds(64 + k, 2, stride=8), :] for k in range(7)]
    for spacing in range(4):
        low = high = None
        for first in range(4 - spacing):
            low_slot = high_slot = None
            for k, weight in enumerate(convolved(first, first + spacing)):
                if weight != 0.0:
                    low_slot = plus(low_slot, weight * low_terms[k])
                    high_slot = plus(high_slot, weight * high_terms[k])
            low = plus(low, roll(low_slot, first, 1))
            high = plus(high, roll(high_slot, first, 1))
        out_ref[spacing * 10 : spacing * 10 + 8, :] = low
        out_ref[spacing * 10 + 8 : spacing * 10 + 10, :] = high


def plus(total, value):
    return value if total is None else total + value


def pair_members(code_ref, pair):
    code = code_ref[0, pair]
    blocks = []
    for shift in (0, 10):
        block = jnp.bitwise_and(lax.shift_right_logical(code, shift), 1023)
        blocks.append((jnp.minimum(block, BLK_DEV - 1), jnp.bitwise_and(block, NO_BLOCK)))
    return lax.shift_right_logical(code, 20), blocks


def pair_codes(window):
    column = lax.shift_right_logical(window, 4) * 2 + jnp.bitwise_and(window, 1)
    hot = (iota((N_COL, BLK_DEV), 0) == column).astype(F32)
    before = (iota((OBS, OBS), 0) < iota((OBS, OBS), 1)).astype(F32).astype(BF16)
    count = jnp.zeros((N_COL, 1), F32)
    ranks = []
    for start in range(0, BLK_DEV, OBS):
        part = hot[:, start : start + OBS]
        seen = jnp.dot(part.astype(BF16), before, preferred_element_type=F32) + count
        ranks.append(jnp.sum(part * seen, axis=0, keepdims=True))
        count = count + jnp.sum(part, axis=1, keepdims=True)
    rank = jnp.concatenate(ranks, axis=1).astype(jnp.int32)
    pairs = lax.shift_right_logical(count.astype(jnp.int32) + 1, 1).astype(F32)
    below = (iota((N_COL, N_COL), 1) < iota((N_COL, N_COL), 0)).astype(F32).astype(BF16)
    spread = jnp.broadcast_to(pairs, (N_COL, OBS)).astype(BF16)
    start = jnp.dot(below, spread, preferred_element_type=F32)[:, :1]
    pair = jnp.sum(hot * start, axis=0, keepdims=True).astype(jnp.int32)
    pair = pair + lax.shift_right_logical(rank, 1)
    second = jnp.bitwise_and(rank, 1)
    missing = NO_BLOCK - iota((1, BLK_DEV), 1)
    high, low = lax.shift_right_logical(missing, 4), jnp.bitwise_and(missing, 15)
    first = 1 - second
    rows = [first * high, first * low, second * high, second * low, first * column]
    rows = jnp.concatenate([row.astype(F32) for row in rows] + [jnp.zeros((11, BLK_DEV), F32)], axis=0)
    target = (iota((CODES, BLK_DEV), 0) == pair).astype(F32).astype(BF16)
    found = lax.dot_general(rows.astype(BF16), target, NT, preferred_element_type=F32)
    found = found.astype(jnp.int32)
    left = NO_BLOCK - found[0:1] * 16 - found[1:2]
    right = NO_BLOCK - found[2:3] * 16 - found[3:4]
    return left + right * 1024 + found[4:5] * (1 << 20)


def knots_hot(knot_ref, block, offset):
    hot = iota((KNOTS, OBS), 0) == knot_ref[pl.ds(block, 1), :] + offset
    return hot.astype(F32).astype(BF16)


def normals_kernel(
    comp_ref,
    phase_ref,
    knot_ref,
    weight_ref,
    list_ref,
    window_row_ref,
    count_ref,
    window_ref,
    out_ref,
    watt_ref,
    code_ref,
    poly_ref,
    pair_ref,
    total_ref,
    joined_ref,
):
    code_ref[...] = pair_codes(window_row_ref[...])
    named = jnp.zeros((16, BLK_DEV // 8), F32)
    capacity = list_ref.shape[1]
    slot = iota((1, capacity), 1)
    for owner in range(N_SRC):
        entry = jnp.where(slot < count_ref[owner], list_ref[owner : owner + 1, :], -1)
        group_hot = iota((BLK_DEV // 8, capacity), 0) == lax.shift_right_arithmetic(entry, 3)
        place_hot = iota((16, capacity), 0) == jnp.where(entry < 0, -1, jnp.bitwise_and(entry, 7))
        named = named + lax.dot_general(
            place_hot.astype(F32).astype(BF16),
            group_hot.astype(F32).astype(BF16),
            NT,
            preferred_element_type=F32,
        )
    named = jnp.concatenate([named[:8], jnp.zeros((8, OBS - BLK_DEV // 8), F32)], axis=1)

    def prepare(group, carry):
        at = pl.ds(pl.multiple_of(group * 8, 8), 8)
        phase = phase_ref[at, :]
        rest = 1.0 - phase
        up = [None, phase, phase * phase, None]
        down = [None, rest, rest * rest, None]
        up[3] = up[2] * phase
        down[3] = down[2] * rest
        poly = [
            down[3] * down[3],
            phase * (down[3] * down[2]),
            up[2] * (down[2] * down[2]),
            up[3] * down[3],
            (up[2] * up[2]) * down[2],
            (up[3] * up[2]) * rest,
            up[3] * up[3],
            jnp.zeros_like(phase),
        ]
        for k in range(8):
            poly_ref[pl.ds(group * 64 + k, 8, stride=8), :] = poly[k]
        times = jnp.take_along_axis(named, jnp.full((8, OBS), group, jnp.int32), axis=1)
        weight = weight_ref[at, :] * times
        watt_ref[at, :] = weight
        comps = [comp_ref[pl.ds(group * 32 + p, 8, stride=4), :] for p in range(4)]
        weighted = [weight * comps[p] for p in range(4)]
        for i, (p, q) in enumerate(PAIRS):
            pair_ref[i, at, :] = weighted[p] * comps[q]
        return carry

    lax.fori_loop(0, BLK_DEV // 8, prepare, 0, unroll=16)
    total_ref[...] = jnp.zeros_like(total_ref)
    unrolled = 128

    def one_group(group, carry):
        for i in range(unrolled):
            block = group * unrolled + i
            poly = poly_ref[pl.ds(pl.multiple_of(block * 8, 8), 8), :]
            terms = jnp.concatenate(
                [poly * pair_ref[n, pl.ds(block, 1), :] for n in range(len(PAIRS))], axis=0
            )
            hot = knots_hot(knot_ref, block, 0)
            summed = lax.dot_general(
                jnp.concatenate(split2(terms), axis=1),
                jnp.concatenate([hot, hot], axis=1),
                NT,
                preferred_element_type=F32,
            )
            column = column_window(window_ref, block)
            total_ref[column] = total_ref[column] + summed
        return carry

    lax.fori_loop(0, BLK_DEV // unrolled, one_group, 0)
    for owner in range(N_SRC):
        joined_ref[owner, :, :] = jnp.concatenate(
            [total_ref[2 * owner], total_ref[2 * owner + 1]], axis=1
        )
    for owner in range(N_SRC):
        fold_bands(joined_ref.at[owner], out_ref.at[owner])


def normal_sums(comps, phase, knots, weight, lists, counts, window):
    return pl.pallas_call(
        normals_kernel,
        out_shape=(
            jax.ShapeDtypeStruct((N_SRC, BAND_ROWS, OBS), F32),
            jax.ShapeDtypeStruct((BLK_DEV, OBS), F32),
            jax.ShapeDtypeStruct((1, CODES), jnp.int32),
        ),
        in_specs=[VMEM] * 6 + [SMEM] * 2,
        out_specs=(VMEM, VMEM, VMEM),
        scratch_shapes=[
            pltpu.VMEM((BLK_DEV * 8, OBS), F32),
            pltpu.VMEM((len(PAIRS), BLK_DEV, OBS), F32),
            pltpu.VMEM((N_COL, PAIR_ROWS, KNOTS), F32),
            pltpu.VMEM((N_SRC, PAIR_ROWS, OBS), F32),
        ],
        compiler_params=params(32),
        cost_estimate=pl.CostEstimate(flops=3_000_000_000, bytes_accessed=4_000_000, transcendentals=0),
        name="normal_sums",
    )(comps, phase, knots, weight, lists, window.reshape(1, BLK_DEV), counts, window)


def solve_five(totals):
    def entry_at(across, within):
        row = across * (across + 1) // 2 + within
        return totals[row : row + 1, :]

    factor = {}
    inverse = {}
    for across in range(5):
        for within in range(across + 1):
            entry = entry_at(across, within)
            if across == within:
                entry = entry + 1.0
            for before in range(within):
                entry = entry - factor[across, before] * factor[within, before]
            if across == within:
                inverse[across] = 1.0 / jnp.sqrt(entry)
            else:
                factor[across, within] = entry * inverse[within]
    forward = []
    for across in range(5):
        entry = totals[15 + across : 16 + across, :]
        for before in range(across):
            entry = entry - factor[across, before] * forward[before]
        forward.append(entry * inverse[across])
    backward = [None] * 5
    for across in range(4, -1, -1):
        entry = forward[across]
        for later in range(across + 1, 5):
            entry = entry - factor[later, across] * backward[later]
        backward[across] = entry * inverse[across]
    return backward


def rights_kernel(
    own_ref,
    near_ref,
    far_ref,
    cross_ref,
    design_ref,
    resid_ref,
    watt_ref,
    comp_ref,
    phase_ref,
    knot_ref,
    source_ref,
    code_ref,
    bands_ref,
    step_ref,
    first_ref,
    sums_ref,
    column_ref,
    term_ref,
    total_ref,
):
    totals = (own_ref[...] + near_ref[...]) + (far_ref[...] + cross_ref[...])
    step = solve_five(totals)
    for p in range(5):
        step_ref[p : p + 1, :] = step[p]
    stacked = jnp.concatenate(step + [jnp.zeros((3, SRC_DEV), F32)], axis=0)
    pieces = jnp.concatenate(list(split3(stacked)) + [jnp.zeros((8, SRC_DEV), BF16)], axis=0)
    local = jnp.bitwise_and(source_ref[...], SRC_DEV - 1)
    hot = (iota((SRC_DEV, BLK_DEV), 0) == local).astype(F32).astype(BF16)
    picked = jnp.dot(pieces, hot, preferred_element_type=F32)
    picked = picked[:8] + picked[8:16] + picked[16:24]
    column_ref[...] = jnp.concatenate([picked, jnp.zeros((OBS - 8, BLK_DEV), F32)], axis=0).T

    def prepare(group, carry):
        at = pl.ds(pl.multiple_of(group * 8, 8), 8)
        columns = column_ref[at, :]
        fitted = jnp.zeros((8, OBS), F32)
        for p in range(5):
            fitted = fitted + design_ref[p, at, :] * columns[:, p : p + 1]
        first = resid_ref[at, :] - fitted
        first_ref[at, :] = first
        weighted = watt_ref[at, :] * first
        spline = spline_weights(phase_ref[at, :])
        comps = [comp_ref[pl.ds(group * 32 + p, 8, stride=4), :] for p in range(4)]
        for m in range(4):
            scaled = weighted * spline[m]
            for p in range(4):
                term_ref[pl.ds(group * 128 + 4 * m + p, 8, stride=16), :] = scaled * comps[p]
        return carry

    lax.fori_loop(0, BLK_DEV // 8, prepare, 0, unroll=64)
    total_ref[...] = jnp.zeros_like(total_ref)
    unrolled = 136

    def one_group(group, carry):
        for i in range(unrolled):
            at, blocks = pair_members(code_ref, group * unrolled + i)
            sides = []
            for block, offset in blocks:
                terms = term_ref[pl.ds(pl.multiple_of(block * 16, 16), 16), :]
                sides.append(
                    (jnp.concatenate(split2(terms), axis=0), knots_hot(knot_ref, block, offset))
                )
            summed = lax.dot_general(
                jnp.concatenate([sides[0][0], sides[1][0]], axis=1),
                jnp.concatenate([sides[0][1], sides[1][1]], axis=1),
                NT,
                preferred_element_type=F32,
            )
            total_ref[at] = total_ref[at] + (summed[:RIGHT_ROWS] + summed[RIGHT_ROWS:])
        return carry

    lax.fori_loop(0, N_PAIR // unrolled, one_group, 0)
    for owner in range(N_SRC):
        joined = jnp.concatenate([total_ref[2 * owner], total_ref[2 * owner + 1]], axis=1)
        right = joined[:4]
        for first in range(1, 4):
            right = right + roll(joined[4 * first : 4 * first + 4], first, 1)
        sums_ref[owner, :BAND_ROWS, :] = bands_ref[owner]
        sums_ref[owner, BAND_ROWS:, :] = jnp.concatenate([right, jnp.zeros((4, OBS), F32)], axis=0)


def right_sums(parts, design, resid, watt, comps, phase, knots, source_row, codes, sums):
    return pl.pallas_call(
        rights_kernel,
        out_shape=(
            jax.ShapeDtypeStruct((5, SRC_DEV), F32),
            jax.ShapeDtypeStruct((BLK_DEV, OBS), F32),
            jax.ShapeDtypeStruct((N_SRC, ROWS, OBS), F32),
        ),
        in_specs=[VMEM] * 11 + [SMEM, VMEM],
        out_specs=(VMEM, VMEM, VMEM),
        scratch_shapes=[
            pltpu.VMEM((BLK_DEV, OBS), F32),
            pltpu.VMEM((BLK_DEV * 16, OBS), F32),
            pltpu.VMEM((N_COL, RIGHT_ROWS, KNOTS), F32),
        ],
        compiler_params=params(32),
        name="right_sums",
    )(*parts, design, resid, watt, comps, phase, knots, source_row, codes, sums)


def solve_kernel(prior, got_ref, out_ref, work_ref):
    total = got_ref[0]
    for other in range(1, N_SRC):
        total = total + got_ref[other]
    lane8 = iota((8, OBS), 1)
    sublane8 = iota((8, OBS), 0)
    index = {}
    for i, (p, q) in enumerate(PAIRS):
        index[p, q] = index[q, p] = i
    bands = []
    for spacing in range(4):
        rows = [total[spacing * 10 + i : spacing * 10 + i + 1] for i in range(10)]
        if spacing == 0:
            rows = [row + prior if PAIRS[i][0] == PAIRS[i][1] else row for i, row in enumerate(rows)]
        full = [rows[index[p, q]] for p in range(4) for q in range(4)]
        bands.append([jnp.concatenate(full[:8], axis=0), jnp.concatenate(full[8:], axis=0)])
    right = total[BAND_ROWS : BAND_ROWS + 4]
    right = jnp.concatenate([right, right], axis=0)

    place = jnp.bitwise_and(lane8, 31)
    window_at = jnp.bitwise_and(lane8, 64)
    is_down = jnp.bitwise_and(lane8, 32) != 0

    def arranged(values, spacing, base):
        step = place + base
        up_index = jnp.minimum(window_at + step, OBS - 1)
        down_index = jnp.maximum(window_at + KNOTS - 1 - step, 0)
        up = jnp.take_along_axis(roll(values, spacing, 1), up_index, axis=1)
        down = jnp.take_along_axis(values, down_index, axis=1)
        down = jnp.where(step - spacing >= HALF, 0.0, down)
        return jnp.where(is_down, down, up)

    def entering(base):
        return [arranged(bands[d][h], d, base) for d in range(4) for h in range(2)] + [
            arranged(right, 0, base)
        ]

    stream, tail = entering(0), entering(32)

    lower = sublane8 < 4

    def insert(front, target, pieces, slot, present):
        def part(d, p, half):
            values = pieces[2 * d + p // 2]
            return values if p % 2 == half else roll(values, 4, 0)

        for d in range(1, present + 1):
            other = (slot - d) % 4
            for q in range(4):
                old = front[other * 4 + q]
                fresh = part(d, q, slot % 2)
                keep = lower if slot % 2 == 1 else jnp.logical_not(lower)
                old[slot // 2] = jnp.where(keep, old[slot // 2], fresh)
        for p in range(4):
            halves = []
            for h in range(2):
                both = []
                for spot in range(2):
                    d = (slot - (2 * h + spot)) % 4
                    both.append(part(d, p, spot) if d <= present else jnp.zeros((8, OBS), F32))
                halves.append(jnp.where(lower, both[0], both[1]))
            front[slot * 4 + p] = halves
        keep = lower if slot % 2 == 1 else jnp.logical_not(lower)
        target[slot // 2] = jnp.where(keep, target[slot // 2], pieces[8])

    def eliminate(front, target, slot, gone):
        scale = None
        for p in range(4):
            row = slot * 4 + p
            half, at = row // 8, row % 8
            column = front[row]
            inverse = 1.0 / column[half][at : at + 1, :]
            scale = inverse if scale is None else jnp.where(sublane8 == at, inverse, scale)
            factor = [column[h] * inverse for h in range(2)]
            factor[half] = jnp.where(sublane8 == at, 0.0, factor[half])
            gone = gone | {row}
            for c in [c for c in range(16) if c not in gone] + [16]:
                values = target if c == 16 else front[c]
                pivot = values[half][at : at + 1, :]
                for h in range(2):
                    values[h] = values[h] - factor[h] * pivot
        return gone, scale

    def save(front, target, slot, step, scale):
        for r in range(1, 4):
            for q in range(4):
                work_ref[step * 13 + (r - 1) * 4 + q] = (
                    front[(slot + r) % 4 * 4 + q][slot // 2] * scale
                )
        work_ref[step * 13 + 12] = target[slot // 2] * scale

    zero = jnp.zeros((8, OBS), F32)
    front = [[zero, zero] for _ in range(16)]
    target = [zero, zero]
    for step in range(4):
        insert(front, target, [roll(values, -step, 1) for values in stream], step, step)
    for step in range(HALF):
        slot = step % 4
        unused, scale = eliminate(front, target, slot, frozenset())
        save(front, target, slot, step, scale)
        source, shift = (stream, step + 4) if step < 28 else (tail, step - 28)
        insert(front, target, [roll(values, -shift, 1) for values in source], slot, 3)

    mirror = jnp.bitwise_xor(lane8, 32)

    def mirrored(values):
        return jnp.take_along_axis(roll(values, 4, 0), mirror, axis=1)

    front = [
        [front[a * 4 + p][h] + mirrored(front[(3 - a) * 4 + p][1 - h]) for h in range(2)]
        for a in range(4)
        for p in range(4)
    ]
    target = [target[h] + mirrored(target[1 - h]) for h in range(2)]
    gone = frozenset()
    scales = {}
    for slot in (2, 3, 0, 1):
        gone, scales[slot] = eliminate(front, target, slot, gone)
    target = [
        target[h] * jnp.where(lower, scales[2 * h], scales[2 * h + 1]) for h in range(2)
    ]

    first_lane = place == 0
    placed = []

    def emit(answer, slot, step):
        values = answer[slot // 2]
        values = values if slot % 2 == 0 else roll(values, 4, 0)
        placed.append(roll(jnp.where(first_lane, values, 0.0), step, 1))

    def back(answer, slot, step):
        half = slot // 2
        parts = [work_ref[step * 13 + 12]]
        for r in (3, 2, 1):
            other = (slot + r) % 4
            terms = []
            for q in range(4):
                at = other % 2 * 4 + q
                terms.append(
                    work_ref[step * 13 + (r - 1) * 4 + q] * answer[other // 2][at : at + 1, :]
                )
            parts.append((terms[0] + terms[1]) + (terms[2] + terms[3]))
        fresh = ((parts[0] - parts[1]) - parts[2]) - parts[3]
        keep = lower if slot % 2 == 1 else jnp.logical_not(lower)
        answer[half] = jnp.where(keep, answer[half], fresh)

    answer = list(target)
    emit(answer, 3, 31)
    emit(answer, 2, 30)
    for step in range(HALF - 1, -1, -1):
        back(answer, step % 4, step)
        emit(answer, step % 4, step)
    while len(placed) > 1:
        placed = [placed[i] + placed[i + 1] for i in range(0, len(placed), 2)]
    result = placed[0]
    knot = jnp.bitwise_and(lane8, KNOTS - 1)
    from_lane = jnp.where(knot < 32, lane8, window_at + 32 + KNOTS - 1 - knot)
    panel = jnp.take_along_axis(result, from_lane, axis=1)
    for owner in range(N_SRC):
        out_ref[owner] = panel[:4]


def solve_panels(got, prior):
    def body(*refs):
        solve_kernel(prior, *refs)

    return pl.pallas_call(
        body,
        out_shape=jax.ShapeDtypeStruct((N_SRC, 4, OBS), F32),
        in_specs=[VMEM],
        out_specs=VMEM,
        scratch_shapes=[pltpu.VMEM((HALF * 13, 8, OBS), F32)],
        compiler_params=params(16),
        name="solve_panels",
    )(got)


def window_hot_kernel(window_ref, hot_ref):
    window = window_ref[...]
    place = jnp.bitwise_and(window, 1) * N_SRC + lax.shift_right_logical(window, 4)
    row = iota((OBS, BLK_DEV), 0)
    hot = (jnp.bitwise_and(row, N_COL - 1) == place) & (row < 3 * N_COL)
    hot_ref[...] = hot.astype(F32).T


def window_hot(window_row):
    return pl.pallas_call(
        window_hot_kernel,
        out_shape=pltpu.VMEM((BLK_DEV, OBS), F32),
        in_specs=[VMEM],
        out_specs=VMEM,
        compiler_params=params(16),
        name="window_hot",
    )(window_row)


def final_kernel(panel_ref, hot_ref, comp_ref, phase_ref, knot_ref, first_ref, out_ref, table_ref):
    sides = []
    for p in range(4):
        even = panel_ref[pl.ds(p, N_SRC, stride=4), :]
        sides.append(jnp.concatenate([even, roll(even, KNOTS, 1)], axis=0))
    pieces = list(split3(jnp.concatenate(sides, axis=1)))
    pieces = jnp.concatenate(pieces + [jnp.zeros((N_COL, 4 * OBS), BF16)], axis=0)
    for start in range(0, BLK_DEV, OBS):
        table_ref[start : start + OBS, :] = jnp.dot(
            hot_ref[start : start + OBS, :].astype(BF16), pieces, preferred_element_type=F32
        )

    def one_group(group, carry):
        at = pl.ds(pl.multiple_of(group * 8, 8), 8)
        knots = knot_ref[at, :]
        spline = spline_weights(phase_ref[at, :])
        correction = [jnp.zeros((8, OBS), F32) for _ in range(4)]
        for p in range(4):
            table = table_ref[at, p * OBS : (p + 1) * OBS]
            comps = comp_ref[pl.ds(group * 32 + p, 8, stride=4), :]
            for m in range(4):
                picked = jnp.take_along_axis(table, knots + m, axis=1, mode="promise_in_bounds")
                correction[m] = correction[m] + comps * picked
        total = spline[0] * correction[0]
        for m in range(1, 4):
            total = total + spline[m] * correction[m]
        out_ref[at, :] = first_ref[at, :] - total
        return carry

    lax.fori_loop(0, BLK_DEV // 8, one_group, 0, unroll=64)


def final_residual(panels, hot, comps, phase, knots, first):
    return pl.pallas_call(
        final_kernel,
        out_shape=jax.ShapeDtypeStruct((BLK_DEV, OBS), F32),
        in_specs=[VMEM] * 6,
        out_specs=VMEM,
        scratch_shapes=[pltpu.VMEM((BLK_DEV, 4 * OBS), F32)],
        compiler_params=params(16),
        name="final_residual",
    )(panels.reshape(N_SRC * 4, OBS), hot, comps, phase, knots, first)


def shards(
    src_design,
    att_comp,
    spline_phase,
    knot_offset,
    obs_weight,
    residual,
    block_source,
    block_window,
    send_list,
    send_count,
):
    n_win = lax.axis_size("win")
    design = src_design.transpose(1, 0, 2)
    comps = att_comp.reshape(BLK_DEV * 4, OBS)
    source_row = block_source.reshape(1, BLK_DEV)
    obs_src = OBS * BLK_DEV * n_win // SRC_DEV
    obs_win = OBS * BLK_DEV // WIN_SUB
    prior = 0.005 * obs_win / obs_src

    def swap(values, bit):
        return lax.ppermute(values, "win", [(i, i ^ bit) for i in range(n_win)])

    stats = source_sums(design, obs_weight, residual, source_row)
    stats = stats + swap(stats, 1)
    parts = (stats, swap(stats, 2), swap(stats, 4), swap(stats, 6))
    sums, watt, codes = normal_sums(
        comps, spline_phase, knot_offset, obs_weight, send_list, send_count, block_window
    )
    source_step, first, sums = right_sums(
        parts,
        design,
        residual,
        watt,
        comps,
        spline_phase,
        knot_offset,
        source_row,
        codes,
        sums,
    )
    got = lax.all_to_all(sums, "src", split_axis=0, concat_axis=0, tiled=True)
    own_panels = solve_panels(got, prior)
    panels = lax.all_to_all(own_panels, "src", split_axis=0, concat_axis=0, tiled=True)
    attitude_step = (
        own_panels[0].reshape(4, WIN_SUB, KNOTS).transpose(1, 2, 0).reshape(WIN_SUB, KNOTS * 4)
    )
    hot = window_hot(block_window.reshape(1, BLK_DEV))
    last = final_residual(panels, hot, comps, spline_phase, knot_offset, first)
    return (source_step, attitude_step, last)


def solution(mesh):
    return jax.shard_map(
        shards,
        mesh=mesh,
        in_specs=(
            P(("src", "win"), None, None),
            P(("src", "win"), None, None),
            P(("src", "win"), None),
            P(("src", "win"), None),
            P(("src", "win"), None),
            P(("src", "win"), None),
            P(("src", "win")),
            P(("src", "win")),
            P(("src", "win"), None),
            P(("src", "win")),
        ),
        out_specs=(P(None, "src"), P(("src", "win"), None), P(("src", "win"), None)),
        check_vma=False,
    )
```
